32 devices in a mesh: lon: 8 (over y, x, core), lat: 4 (over z).
Axes of the slice: x: 2, y: 2, z: 4, core: 2. Of those that a mesh axis runs over, the one named last changes fastest.
Arguments:
- coarse: bfloat16 [12, 8, 8192], P(None, None, ('lon', 'lat')), may hold values from -6 to 6
- target: float32 [4, 8, 8192], P(None, 'lat', 'lon'), may hold values from -6 to 6
- noise: float32 [4, 8, 8192], P(None, 'lat', 'lon'), may hold values from -6 to 6
- land_mask: int32 [8, 8192], P('lat', 'lon'), may hold values 0 or 1
- level_index: int32 [4, 8], P('lat', 'lon'), may hold values from 0 to 31
- frozen_first: bfloat16 [3, 3, 128, 12], replicated, may hold values from -0.625 to 0.625
- frozen_middle: bfloat16 [3, 3, 128, 128], replicated, may hold values from -0.1875 to 0.1875
- frozen_last: bfloat16 [3, 3, 4, 128], replicated, may hold values from -0.1875 to 0.1875
- diffuse_in: bfloat16 [3, 3, 128, 20], replicated, may hold values from -0.4375 to 0.4375
- diffuse_down: bfloat16 [3, 3, 256, 128], replicated, may hold values from -0.1875 to 0.1875
- diffuse_up: bfloat16 [3, 3, 128, 256], replicated, may hold values from -0.125 to 0.125
- diffuse_out: bfloat16 [3, 3, 4, 128], replicated, may hold values from -0.1875 to 0.1875
Outputs:
- denoised: float32 [4, 8, 8192], P(None, 'lat', 'lon')
- grad_in: float32 [3, 3, 128, 20], replicated
- grad_down: float32 [3, 3, 256, 128], replicated
- grad_up: float32 [3, 3, 128, 256], replicated
- grad_last: float32 [3, 3, 4, 128], replicated
The draws below stay inside these ranges and needn't reach their ends.
All inputs are finite; a program needn't handle non-finite values. No bound on the sum of `land_mask` on one device may be relied on, other than what follows from the above.
Results may differ from the reference program's by a relative error of at most 0.0044.
Values may be sent and summed in bfloat16 or wider, within the bound.
A program may use at most 128 MiB of HBM per device.

```python
import math
import jax
import jax.numpy as jnp
from jax import lax

C_IN = 12
C_OUT = 4
HID1 = 128
HID2 = 256
LEVELS = 32
LAT_DEV = 2
LON_DEV = 1024
CAT = 20
NLAT = 8
NLON = 8192
N_LON = 8
N_LAT = 4


def place_ends(values, own_key, low, high):
    longest = values.shape.index(max(values.shape))
    spots = []
    for shift in (0, 1):
        where = [jax.random.randint(jax.random.fold_in(own_key, axis), (), 0, length) for axis, length in enumerate(values.shape)]
        where[longest] = (where[longest] + shift) % values.shape[longest]
        spots.append(tuple(where))
    return values.at[spots[0]].set(low).at[spots[1]].set(high)


def shard_levels(own_key, shape, split, least, top_value):
    loudness, own = 1.0, jax.random.fold_in(own_key, 6)
    for position, shards_of in split:
        draws = jnp.exp(jax.random.uniform(jax.random.fold_in(own, position), (shards_of,), jnp.float32, least / len(split), top_value / len(split)))
        loudness = loudness * jnp.repeat(draws, shape[position] // shards_of).reshape([-1 if axis == position else 1 for axis in range(len(shape))])
    return loudness


def scatter_about(rng, shape, width, limit, pieces=(), held_as=jnp.bfloat16):
    result = jax.random.normal(rng, shape, jnp.float32) * width
    if len(pieces) > 0:
        result = shard_levels(rng, shape, pieces, -0.22, 0.18) * result
    return jnp.clip(result, min=-limit, max=limit).astype(held_as)


def setup_inputs(seed: int = 0) -> dict:
    keys = jax.random.split(jax.random.key(seed), 13)
    return {
        "coarse": scatter_about(keys[0], (C_IN, NLAT, NLON), 1.0, 6.0, ((2, 32),)),
        "target": scatter_about(keys[1], (C_OUT, NLAT, NLON), 1.0, 6.0, ((1, 4), (2, 8)), jnp.float32),
        "noise": scatter_about(keys[2], (C_OUT, NLAT, NLON), 1.0, 6.0, ((1, 4), (2, 8)), jnp.float32),
        "land_mask": place_ends((jax.random.randint(keys[3], (NLAT, NLON), 0, 10) < 3).astype(jnp.int32), jax.random.fold_in(keys[3], 1), 0, 1),
        "level_index": place_ends(jax.random.randint(keys[4], (N_LAT, N_LON), 0, LEVELS), jax.random.fold_in(keys[4], 1), 0, LEVELS - 1).astype(jnp.int32),
        "frozen_first": scatter_about(keys[5], (3, 3, HID1, C_IN), (9 * C_IN) ** -0.5, 0.625),
        "frozen_middle": scatter_about(keys[6], (3, 3, HID1, HID1), (9 * HID1) ** -0.5, 0.1875),
        "frozen_last": scatter_about(keys[7], (3, 3, C_OUT, HID1), (9 * HID1) ** -0.5, 0.1875),
        "diffuse_in": scatter_about(keys[8], (3, 3, HID1, CAT), (9 * CAT) ** -0.5, 0.4375),
        "diffuse_down": scatter_about(keys[9], (3, 3, HID2, HID1), (9 * HID1) ** -0.5, 0.1875),
        "diffuse_up": scatter_about(keys[10], (3, 3, HID1, HID2), (9 * HID2) ** -0.5, 0.125),
        "diffuse_out": scatter_about(keys[11], (3, 3, C_OUT, HID1), (9 * HID1) ** -0.5, 0.1875),
    }


def conv_valid(padded, weight):
    height = padded.shape[1] - 2
    breadth = padded.shape[2] - 2
    total = jnp.zeros((weight.shape[2], height * breadth), jnp.float32)
    for row_tap in range(3):
        for col_tap in range(3):
            tile = padded[:, row_tap:row_tap + height, col_tap:col_tap + breadth].reshape(padded.shape[0], height * breadth)
            total = total + jnp.dot(weight[row_tap, col_tap], tile, preferred_element_type=jnp.float32)
    return total.reshape(weight.shape[2], height, breadth)

def weight_grad(padded, cotangent):
    outer = cotangent.shape[0]
    height = cotangent.shape[1]
    breadth = cotangent.shape[2]
    flat = cotangent.reshape(outer, height * breadth)
    taps = []
    for row_tap in range(3):
        for col_tap in range(3):
            tile = padded[:, row_tap:row_tap + height, col_tap:col_tap + breadth].reshape(padded.shape[0], height * breadth)
            taps.append(lax.dot_general(flat, tile, (((1,), (1,)), ((), ())), preferred_element_type=jnp.float32))
    return jnp.stack(taps, 0).reshape(3, 3, outer, padded.shape[0])

def input_grad(padded, weight):
    height = padded.shape[1] - 2
    breadth = padded.shape[2] - 2
    total = jnp.zeros((weight.shape[3], height * breadth), jnp.float32)
    for row_tap in range(3):
        for col_tap in range(3):
            tile = padded[:, row_tap:row_tap + height, col_tap:col_tap + breadth].reshape(padded.shape[0], height * breadth)
            total = total + jnp.dot(weight[2 - row_tap, 2 - col_tap].T, tile, preferred_element_type=jnp.float32)
    return total.reshape(weight.shape[3], height, breadth)

def silu_grad(pre):
    sigmo = jax.nn.sigmoid(pre)
    return sigmo * (1.0 + pre * (1.0 - sigmo))

def regression(inputs, frozen_first, frozen_middle, frozen_last, widen):
    first = jax.nn.silu(conv_valid(widen(inputs), frozen_first)).astype(jnp.bfloat16)
    second = jax.nn.silu(conv_valid(widen(first), frozen_middle)).astype(jnp.bfloat16)
    return conv_valid(widen(second), frozen_last).astype(jnp.bfloat16)

def train_step(mean, coarse_tile, target, noise, land_mask, sigma, diffuse_in, diffuse_down, diffuse_up, diffuse_out, widen, scale, reduce_fn):
    residual = target - mean.astype(jnp.float32)
    noisy = residual + sigma * noise
    variance = sigma * sigma + 0.25
    c_in = lax.rsqrt(variance)
    c_skip = 0.25 / variance
    c_out = 0.5 * sigma * c_in
    lam = variance / (0.25 * sigma * sigma)
    net_in = jnp.concatenate([mean, (c_in * noisy).astype(jnp.bfloat16), coarse_tile], 0)
    pad_in = widen(net_in)
    pre_a = conv_valid(pad_in, diffuse_in)
    act_a = jax.nn.silu(pre_a).astype(jnp.bfloat16)
    chan_one = act_a.shape[0]
    height = act_a.shape[1]
    breadth = act_a.shape[2]
    pooled = act_a.astype(jnp.float32).reshape(chan_one, height // 2, 2, breadth // 2, 2).mean((2, 4)).astype(jnp.bfloat16)
    pad_pool = widen(pooled)
    pre_b = conv_valid(pad_pool, diffuse_down)
    act_b = jax.nn.silu(pre_b).astype(jnp.bfloat16)
    chan_two = act_b.shape[0]
    upsampled = jnp.broadcast_to(act_b[:, :, None, :, None], (chan_two, height // 2, 2, breadth // 2, 2)).reshape(chan_two, height, breadth)
    pad_up = widen(upsampled)
    pre_c = conv_valid(pad_up, diffuse_up)
    act_c = (jax.nn.silu(pre_c) + act_a.astype(jnp.float32)).astype(jnp.bfloat16)
    pad_c = widen(act_c)
    field = conv_valid(pad_c, diffuse_out)
    denoised = c_skip * noisy + c_out * field
    weight_map = 1.0 + land_mask.astype(jnp.float32)
    loss_grad = 2.0 * scale * weight_map * lam * (denoised - residual)
    grad_f = (c_out * loss_grad).astype(jnp.bfloat16)
    grad_last = reduce_fn(weight_grad(pad_c, grad_f))
    back_c = input_grad(widen(grad_f), diffuse_out)
    grad_pre_c = (back_c * silu_grad(pre_c)).astype(jnp.bfloat16)
    grad_up = reduce_fn(weight_grad(pad_up, grad_pre_c))
    back_up = input_grad(widen(grad_pre_c), diffuse_up)
    back_b = back_up.reshape(chan_two, height // 2, 2, breadth // 2, 2).sum((2, 4))
    grad_pre_b = (back_b * silu_grad(pre_b)).astype(jnp.bfloat16)
    grad_down = reduce_fn(weight_grad(pad_pool, grad_pre_b))
    back_pool = input_grad(widen(grad_pre_b), diffuse_down)
    spread = jnp.broadcast_to(back_pool[:, :, None, :, None], (chan_one, height // 2, 2, breadth // 2, 2)).reshape(chan_one, height, breadth)
    back_a = back_c + 0.25 * spread
    grad_pre_a = (back_a * silu_grad(pre_a)).astype(jnp.bfloat16)
    grad_in = reduce_fn(weight_grad(pad_in, grad_pre_a))
    return (denoised, (grad_in, grad_down, grad_up, grad_last))

def widen_global(field):
    wrapped = jnp.concatenate([field[:, :, -1:], field, field[:, :, :1]], axis=2)
    return jnp.pad(wrapped, ((0, 0), (1, 1), (0, 0)))

def keep_same(value):
    return value

def reference(coarse, target, noise, land_mask, level_index, frozen_first, frozen_middle, frozen_last, diffuse_in, diffuse_down, diffuse_up, diffuse_out):
    mean = regression(coarse, frozen_first, frozen_middle, frozen_last, widen_global)
    tile_sigma = 0.02 * 4000.0 ** (level_index.astype(jnp.float32) / (LEVELS - 1))
    sigma = jnp.broadcast_to(tile_sigma[:, None, :, None], (N_LAT, LAT_DEV, N_LON, LON_DEV)).reshape(NLAT, NLON)[None]
    scale = 1.0 / (C_OUT * math.sqrt(NLAT * NLON))
    denoised, grads = train_step(mean, coarse, target, noise, land_mask, sigma, diffuse_in, diffuse_down, diffuse_up, diffuse_out, widen_global, scale, keep_same)
    return (denoised, grads[0], grads[1], grads[2], grads[3])
```

```python
import functools
import math

import jax
import jax.numpy as jnp
from jax import lax
from jax.experimental import pallas as pl
from jax.experimental.pallas import tpu as pltpu
from jax.sharding import PartitionSpec as P

LEVELS = 32
EDGE = 16
HALF = EDGE // 2
F32 = jnp.float32
BF16 = jnp.bfloat16


def dot_nt(x, y):
    return lax.dot_general(x, y, (((1,), (1,)), ((), ())), preferred_element_type=F32)


def dot_tn(x, y):
    return lax.dot_general(x, y, (((0,), (0,)), ((), ())), preferred_element_type=F32)


def dot_nn(x, y):
    return jnp.dot(x, y, preferred_element_type=F32)


def sigmoid(v):
    return 1.0 / (1.0 + jnp.exp(-v))


def roll(x, amount, axis):
    size = x.shape[axis]
    return pltpu.roll(x, amount % size, axis)


def kernel(
    rows, span, scale,
    coarse_ref, packed_ref, first_ref, middle_ref, last_ref, in_ref, down_ref, up_ref, out_ref,
    den_ref, gin_ref, gdown_ref, gup_ref, glast_ref,
    fine, pre_a, act_a, pool, pre_b, deep, pre_c, act_c, back, weff, net,
):
    cells = rows * span
    low = rows // 2
    lcells = low * span
    lane = lax.broadcasted_iota(jnp.int32, (1, cells), 1)
    row_of = lane // span
    col_of = lane - row_of * span
    own = (col_of >= HALF) & (col_of < span - HALF)
    col_l = lax.broadcasted_iota(jnp.int32, (lcells, 1), 0) % span
    own_l = (col_l >= HALF) & (col_l < span - HALF)
    col_f = lax.broadcasted_iota(jnp.int32, (cells, 1), 0) % span
    own_f = (col_f >= HALF) & (col_f < span - HALF)

    def row_shift(x, step):
        if step == 0:
            return x
        ok = (row_of + step >= 0) & (row_of + step < rows)
        return jnp.where(ok, roll(x, -step * span, 1), 0.0)

    def col_sources(even, odd):
        return [roll(odd, 1, 1), even, odd, roll(even, -1, 1)]

    def taps(even, odd):
        src = col_sources(even, odd)
        return [[row_shift(s, a - 1) for s in src] for a in range(3)]

    def unfold(table, plane):
        parts = [table[a][plane + b] for a in range(3) for b in range(3)]
        return jnp.concatenate(parts, 0).astype(BF16)

    def unfold_back(table, plane):
        parts = [table[2 - a][plane + 2 - b] for a in range(3) for b in range(3)]
        return jnp.concatenate(parts, 0).astype(BF16)

    def narrow_conv(x_even, x_odd, w):
        ys = (dot_nt(w, x_even), dot_nt(w, x_odd))
        outs = []
        for plane in range(2):
            total = None
            for a in range(3):
                part = None
                for b in range(3):
                    k = plane + b
                    y = ys[(k + 1) % 2][(3 * a + b) * 8 : (3 * a + b) * 8 + 8]
                    if k == 0:
                        y = roll(y, 1, 1)
                    if k == 3:
                        y = roll(y, -1, 1)
                    part = y if part is None else part + y
                part = row_shift(part, a - 1)
                total = part if total is None else total + part
            outs.append(total)
        return outs

    def store_fine(even, odd):
        for k, v in enumerate((roll(odd, 1, 0), even, odd, roll(even, -1, 0))):
            fine[span : span + cells, 128 * k : 128 * k + 128] = v.astype(BF16)

    def store_low(ref, v):
        c = v.shape[1]
        for k, s in enumerate((roll(v, 1, 0), v, roll(v, -1, 0))):
            ref[span : span + lcells, c * k : c * k + c] = s.astype(BF16)

    for ref, count in ((fine, rows), (pool, low), (deep, low)):
        zero = jnp.zeros((span, ref.shape[1]), BF16)
        ref[0:span, :] = zero
        ref[(count + 1) * span : (count + 2) * span, :] = zero

    coarse = (coarse_ref[0], coarse_ref[1])
    table = taps(*coarse)
    first = []
    for plane in range(2):
        v = dot_tn(unfold(table, plane), first_ref[...])
        first.append((v * sigmoid(v)).astype(BF16).astype(F32))
    store_fine(*first)
    second = []
    for plane in range(2):
        v = None
        for a in range(3):
            w = jnp.concatenate([middle_ref[a, b] for b in range(3)], 1)
            d = dot_nt(fine[a * span : a * span + cells, 128 * plane : 128 * plane + 384], w)
            v = d if v is None else v + d
        second.append((v * sigmoid(v)).astype(BF16))
    mean = [m.astype(BF16).astype(F32) for m in narrow_conv(second[0], second[1], last_ref[...])]

    residual, noisy, sigma, mixed = [], [], [], []
    for plane in range(2):
        sig = packed_ref[plane, 17:18]
        res = packed_ref[plane, 0:8] - mean[plane]
        noi = res + sig * packed_ref[plane, 8:16]
        c_in = lax.rsqrt(sig * sig + 0.25)
        scaled = (c_in * noi).astype(BF16).astype(F32)
        mixed.append(jnp.concatenate([mean[plane] + roll(scaled, 4, 0), coarse[plane]], 0))
        residual.append(res)
        noisy.append(noi)
        sigma.append(sig)
    table = taps(*mixed)
    for plane in range(2):
        net[plane] = unfold(table, plane)
        v = dot_tn(net[plane], in_ref[...])
        pre_a[plane] = v
        act_a[plane] = (v * sigmoid(v)).astype(BF16)

    parts = []
    for i in range(low):
        total = None
        for r in (2 * i, 2 * i + 1):
            for plane in range(2):
                v = act_a[plane, r * span : (r + 1) * span].astype(F32)
                total = v if total is None else total + v
        parts.append(0.25 * total)
    store_low(pool, jnp.concatenate(parts, 0).astype(BF16).astype(F32))
    v = None
    for a in range(3):
        w = jnp.concatenate([down_ref[a, b] for b in range(3)], 1)
        d = dot_nt(pool[a * span : a * span + lcells, :], w)
        v = d if v is None else v + d
    pre_b[...] = v
    store_low(deep, (v * sigmoid(v)).astype(BF16).astype(F32))

    groups = (((0,), (1, 2)), ((0, 1), (2,)))
    for pr in range(2):
        for pc in range(2):
            for rho in range(2):
                for gam in range(2):
                    w = None
                    for a in groups[pr][rho]:
                        for b in groups[pc][gam]:
                            u = up_ref[a, b].astype(F32)
                            w = u if w is None else w + u
                    weff[pr, pc, rho, :, 256 * gam : 256 * gam + 256] = w.astype(BF16)
    for pr in range(2):
        for pc in range(2):
            v = None
            for rho in range(2):
                at = (pr + rho) * span
                d = dot_nt(deep[at : at + lcells, 256 * pc : 256 * pc + 512], weff[pr, pc, rho])
                v = d if v is None else v + d
            s = v * sigmoid(v)
            for i in range(low):
                r = 2 * i + pr
                here = slice(r * span, (r + 1) * span)
                there = slice(i * span, (i + 1) * span)
                pre_c[pc, here] = v[there]
                act_c[pc, here] = (s[there] + act_a[pc, here].astype(F32)).astype(BF16)

    field = narrow_conv(act_c[0], act_c[1], out_ref[...])
    grad_f = []
    for plane in range(2):
        sig = sigma[plane]
        var = sig * sig + 0.25
        c_out = 0.5 * sig * lax.rsqrt(var)
        den = (0.25 / var) * noisy[plane] + c_out * field[plane]
        den_ref[plane] = den
        weight = 1.0 + packed_ref[plane, 16:17]
        lam = var / (0.25 * sig * sig)
        loss_grad = 2.0 * scale * weight * lam * (den - residual[plane])
        grad_f.append((c_out * loss_grad).astype(BF16).astype(F32))
    table = taps(*[jnp.where(own, g, 0.0) for g in grad_f])
    glast_ref[...] = dot_nn(unfold_back(table, 0), act_c[0]) + dot_nn(unfold_back(table, 1), act_c[1])
    table = taps(*grad_f)
    grad_c = []
    for plane in range(2):
        v = dot_tn(unfold_back(table, plane), out_ref[...])
        back[plane] = v
        pre = pre_c[plane]
        s = sigmoid(pre)
        grad_c.append((v * (s * (1.0 + pre * (1.0 - s)))).astype(BF16).astype(F32))
    store_fine(*grad_c)

    sums = {}
    for pr in range(2):
        for pc in range(2):
            g = jnp.concatenate([grad_c[pc][(2 * i + pr) * span : (2 * i + pr + 1) * span] for i in range(low)], 0)
            g = jnp.where(own_l, g, 0.0).T.astype(BF16)
            for rho in range(2):
                at = (pr + rho) * span
                d = dot_nn(g, deep[at : at + lcells, 256 * pc : 256 * pc + 512])
                for gam in range(2):
                    part = d[:, 256 * gam : 256 * gam + 256]
                    for a in groups[pr][rho]:
                        for b in groups[pc][gam]:
                            if (a, b) in sums:
                                gup_ref[a, b] += part
                            else:
                                sums[(a, b)] = True
                                gup_ref[a, b] = part

    order = ((1, 1), (0, 1), (1, 0), (0, 0))
    v = None
    for k in range(4):
        pr, rho = ((1, 1), (0, 1), (1, 0), (0, 0))[k]
        x = jnp.concatenate([fine[(2 * i + k) * span : (2 * i + k + 1) * span, :] for i in range(low)], 0)
        w = jnp.concatenate([weff[pr, pc, rho, :, 256 * gam : 256 * gam + 256] for pc, gam in order], 0)
        d = dot_nn(x, w)
        v = d if v is None else v + d
    pre = pre_b[...]
    s = sigmoid(pre)
    grad_b = (v * (s * (1.0 + pre * (1.0 - s)))).astype(BF16).astype(F32)
    store_low(deep, grad_b)
    g = jnp.where(own_l, grad_b, 0.0).T.astype(BF16)
    for a in range(3):
        d = dot_nn(g, pool[a * span : a * span + lcells, :])
        for b in range(3):
            gdown_ref[a, b] = d[:, 128 * b : 128 * b + 128]

    v = None
    for a in range(3):
        w = jnp.concatenate([down_ref[a, b] for b in (2, 1, 0)], 0)
        d = dot_nn(deep[(2 - a) * span : (2 - a) * span + lcells, :], w)
        v = d if v is None else v + d
    v = 0.25 * v
    total = None
    for plane in range(2):
        spread = jnp.concatenate([v[(r // 2) * span : (r // 2 + 1) * span] for r in range(rows)], 0)
        pre = pre_a[plane]
        s = sigmoid(pre)
        g = (back[plane] + spread) * (s * (1.0 + pre * (1.0 - s)))
        g = jnp.where(own_f, g, 0.0).astype(BF16)
        d = dot_nn(net[plane], g)
        total = d if total is None else total + d
    gin_ref[...] = total


def compute(rows, span, scale, args):
    cells = rows * span
    low = rows // 2
    lcells = low * span
    vmem = pl.BlockSpec(memory_space=pltpu.VMEM)
    return pl.pallas_call(
        functools.partial(kernel, rows, span, scale),
        out_shape=(
            jax.ShapeDtypeStruct((2, 8, cells), F32),
            jax.ShapeDtypeStruct((216, 128), F32),
            jax.ShapeDtypeStruct((3, 3, 256, 128), F32),
            jax.ShapeDtypeStruct((3, 3, 128, 256), F32),
            jax.ShapeDtypeStruct((72, 128), F32),
        ),
        in_specs=[vmem] * len(args),
        out_specs=(vmem,) * 5,
        scratch_shapes=[
            pltpu.VMEM((cells + 2 * span, 512), BF16),
            pltpu.VMEM((2, cells, 128), F32),
            pltpu.VMEM((2, cells, 128), BF16),
            pltpu.VMEM((lcells + 2 * span, 384), BF16),
            pltpu.VMEM((lcells, 256), F32),
            pltpu.VMEM((lcells + 2 * span, 768), BF16),
            pltpu.VMEM((2, cells, 128), F32),
            pltpu.VMEM((2, cells, 128), BF16),
            pltpu.VMEM((2, cells, 128), F32),
            pltpu.VMEM((2, 2, 2, 128, 512), BF16),
            pltpu.VMEM((2, 216, cells), BF16),
        ],
        compiler_params=pltpu.CompilerParams(vmem_limit_bytes=48 * 1024 * 1024),
    )(*args)


def ring(axis, step):
    count = lax.axis_size(axis)
    return [(i, (i + step) % count) for i in range(count)]


def widen(x, axis):
    head = x[..., :EDGE]
    tail = x[..., -EDGE:]
    left = lax.ppermute(tail, axis, ring(axis, 1))
    right = lax.ppermute(head, axis, ring(axis, -1))
    return jnp.concatenate([left, x, right], -1)


def planes(x):
    c, r, w = x.shape
    return x.reshape(c, r, w // 2, 2).transpose(3, 0, 1, 2).reshape(2, c, r * (w // 2))


def tall(w, channels):
    w = jnp.pad(w.transpose(0, 1, 3, 2), ((0, 0), (0, 0), (0, channels - w.shape[3]), (0, 0)))
    return w.reshape(9 * channels, w.shape[3])


def flat(w):
    return jnp.pad(w, ((0, 0), (0, 0), (0, 8 - w.shape[2]), (0, 0))).reshape(72, w.shape[3])


def local(
    coarse, target, noise, land_mask, level_index,
    frozen_first, frozen_middle, frozen_last, diffuse_in, diffuse_down, diffuse_up, diffuse_out,
):
    n_lat = lax.axis_size("lat")
    rows = coarse.shape[1]
    strip = coarse.shape[2]
    height, breadth = target.shape[1], target.shape[2]
    sigma = 0.02 * 4000.0 ** (level_index.astype(F32) / (LEVELS - 1))
    sigma = jnp.broadcast_to(sigma[None], (1, height, breadth))
    packed = jnp.concatenate([target, noise, land_mask.astype(F32)[None], sigma], 0)
    packed = widen(packed, "lon")
    windows = jnp.stack([packed[:, :, i * strip : i * strip + strip + 2 * EDGE] for i in range(n_lat)], 0)
    windows = lax.all_to_all(windows, "lat", split_axis=0, concat_axis=0, tiled=True)
    packed = windows.transpose(1, 0, 2, 3).reshape(10, rows, strip + 2 * EDGE)
    pad = jnp.zeros((4, rows, strip + 2 * EDGE), F32)
    packed = planes(jnp.concatenate([packed[:4], pad, packed[4:8], pad, packed[8:], pad, pad[:2]], 0))
    wide = widen(coarse, ("lon", "lat")).astype(F32)
    wide = planes(jnp.pad(wide, ((0, 16 - wide.shape[0]), (0, 0), (0, 0))))
    span = strip // 2 + 2 * HALF
    scale = 1.0 / (target.shape[0] * math.sqrt(height * n_lat * breadth * lax.axis_size("lon")))
    den, gin, gdown, gup, glast = compute(
        rows, span, scale,
        (
            wide, packed, tall(frozen_first, 16), frozen_middle, flat(frozen_last),
            tall(diffuse_in, 24), diffuse_down, diffuse_up, flat(diffuse_out),
        ),
    )
    den = den.reshape(2, 8, rows, span)[:, :4, :, HALF : span - HALF]
    den = den.transpose(1, 2, 3, 0).reshape(4, rows, strip)
    den = lax.all_to_all(den, "lat", split_axis=1, concat_axis=2, tiled=True)
    gin, gdown, gup, glast = reduce_all(gin, gdown, gup, glast)
    gin = gin.reshape(3, 3, 24, 128)[:, :, : diffuse_in.shape[3]].transpose(0, 1, 3, 2)
    glast = glast.reshape(3, 3, 8, 128)[:, :, :4]
    return den, gin, gdown, gup, glast


def reduce_all(*grads):
    return lax.psum(grads, ("lon", "lat"))


def solution(mesh):
    return jax.shard_map(
        local,
        mesh=mesh,
        in_specs=(
            P(None, None, ("lon", "lat")),
            P(None, "lat", "lon"),
            P(None, "lat", "lon"),
            P("lat", "lon"),
            P("lat", "lon"),
            P(), P(), P(), P(), P(), P(), P(),
        ),
        out_specs=(P(None, "lat", "lon"), P(), P(), P(), P()),
        check_vma=False,
    )
```

```python
import functools
import math

import jax
import jax.numpy as jnp
from jax import lax
from jax.experimental import pallas as pl
from jax.experimental.pallas import tpu as pltpu
from jax.sharding import PartitionSpec as P

LEVELS = 32
EDGE = 16
HALF = EDGE // 2
AT_UP = 9 * 256
AT_IN = AT_UP + 9 * 256
AT_LAST = AT_IN + 216
AT_END = AT_LAST + 72
F32 = jnp.float32
BF16 = jnp.bfloat16


def dot_nt(x, y):
    return lax.dot_general(x, y, (((1,), (1,)), ((), ())), preferred_element_type=F32)


def dot_tn(x, y):
    return lax.dot_general(x, y, (((0,), (0,)), ((), ())), preferred_element_type=F32)


def dot_nn(x, y):
    return jnp.dot(x, y, preferred_element_type=F32)


def sigmoid(v):
    return 1.0 / (1.0 + jnp.exp(-v))


def roll(x, amount, axis):
    size = x.shape[axis]
    return pltpu.roll(x, amount % size, axis)


def kernel(
    rows, span, scale,
    coarse_ref, packed_ref, first_ref, middle_ref, last_ref, in_ref, down_ref, up_ref, out_ref,
    den_ref, grad_ref,
    fine, pre_a, act_a, pool, pre_b, deep, pre_c, act_c, back, weff, net,
):
    cells = rows * span
    low = rows // 2
    lcells = low * span
    lane = lax.broadcasted_iota(jnp.int32, (1, cells), 1)
    row_of = lane // span
    col_of = lane - row_of * span
    own = (col_of >= HALF) & (col_of < span - HALF)
    col_l = lax.broadcasted_iota(jnp.int32, (lcells, 1), 0) % span
    own_l = (col_l >= HALF) & (col_l < span - HALF)
    col_f = lax.broadcasted_iota(jnp.int32, (cells, 1), 0) % span
    own_f = (col_f >= HALF) & (col_f < span - HALF)

    def row_shift(x, step):
        if step == 0:
            return x
        ok = (row_of + step >= 0) & (row_of + step < rows)
        return jnp.where(ok, roll(x, -step * span, 1), 0.0)

    def col_sources(even, odd):
        return [roll(odd, 1, 1), even, odd, roll(even, -1, 1)]

    def taps(even, odd):
        src = col_sources(even, odd)
        return [[row_shift(s, a - 1) for s in src] for a in range(3)]

    def unfold(table, plane):
        parts = [table[a][plane + b] for a in range(3) for b in range(3)]
        return jnp.concatenate(parts, 0).astype(BF16)

    def unfold_back(table, plane):
        parts = [table[2 - a][plane + 2 - b] for a in range(3) for b in range(3)]
        return jnp.concatenate(parts, 0).astype(BF16)

    def narrow_conv(x_even, x_odd, w):
        ys = (dot_nt(w, x_even), dot_nt(w, x_odd))
        outs = []
        for plane in range(2):
            total = None
            for a in range(3):
                part = None
                for b in range(3):
                    k = plane + b
                    y = ys[(k + 1) % 2][(3 * a + b) * 8 : (3 * a + b) * 8 + 8]
                    if k == 0:
                        y = roll(y, 1, 1)
                    if k == 3:
                        y = roll(y, -1, 1)
                    part = y if part is None else part + y
                part = row_shift(part, a - 1)
                total = part if total is None else total + part
            outs.append(total)
        return outs

    def store_fine(even, odd):
        for k, v in enumerate((roll(odd, 1, 0), even, odd, roll(even, -1, 0))):
            fine[span : span + cells, 128 * k : 128 * k + 128] = v.astype(BF16)

    def store_low(ref, v):
        c = v.shape[1]
        for k, s in enumerate((roll(v, 1, 0), v, roll(v, -1, 0))):
            ref[span : span + lcells, c * k : c * k + c] = s.astype(BF16)

    for ref, count in ((fine, rows), (pool, low), (deep, low)):
        zero = jnp.zeros((span, ref.shape[1]), BF16)
        ref[0:span, :] = zero
        ref[(count + 1) * span : (count + 2) * span, :] = zero

    coarse = (coarse_ref[0], coarse_ref[1])
    table = taps(*coarse)
    first = []
    for plane in range(2):
        v = dot_tn(unfold(table, plane), first_ref[...])
        first.append((v * sigmoid(v)).astype(BF16).astype(F32))
    store_fine(*first)
    second = []
    for plane in range(2):
        v = None
        for a in range(3):
            w = jnp.concatenate([middle_ref[a, b] for b in range(3)], 1)
            d = dot_nt(fine[a * span : a * span + cells, 128 * plane : 128 * plane + 384], w)
            v = d if v is None else v + d
        second.append((v * sigmoid(v)).astype(BF16))
    mean = [m.astype(BF16).astype(F32) for m in narrow_conv(second[0], second[1], last_ref[...])]

    residual, noisy, sigma, mixed = [], [], [], []
    for plane in range(2):
        sig = packed_ref[plane, 17:18]
        res = packed_ref[plane, 0:8] - mean[plane]
        noi = res + sig * packed_ref[plane, 8:16]
        c_in = lax.rsqrt(sig * sig + 0.25)
        scaled = (c_in * noi).astype(BF16).astype(F32)
        mixed.append(jnp.concatenate([mean[plane] + roll(scaled, 4, 0), coarse[plane]], 0))
        residual.append(res)
        noisy.append(noi)
        sigma.append(sig)
    table = taps(*mixed)
    for plane in range(2):
        net[plane] = unfold(table, plane)
        v = dot_tn(net[plane], in_ref[...])
        pre_a[plane] = v
        act_a[plane] = (v * sigmoid(v)).astype(BF16)

    parts = []
    for i in range(low):
        total = None
        for r in (2 * i, 2 * i + 1):
            for plane in range(2):
                v = act_a[plane, r * span : (r + 1) * span].astype(F32)
                total = v if total is None else total + v
        parts.append(0.25 * total)
    store_low(pool, jnp.concatenate(parts, 0).astype(BF16).astype(F32))
    v = None
    for a in range(3):
        w = jnp.concatenate([down_ref[a, b] for b in range(3)], 1)
        d = dot_nt(pool[a * span : a * span + lcells, :], w)
        v = d if v is None else v + d
    pre_b[...] = v
    store_low(deep, (v * sigmoid(v)).astype(BF16).astype(F32))

    groups = (((0,), (1, 2)), ((0, 1), (2,)))
    for pr in range(2):
        for pc in range(2):
            for rho in range(2):
                for gam in range(2):
                    w = None
                    for a in groups[pr][rho]:
                        for b in groups[pc][gam]:
                            u = up_ref[a, b].astype(F32)
                            w = u if w is None else w + u
                    weff[pr, pc, rho, :, 256 * gam : 256 * gam + 256] = w.astype(BF16)
    for pr in range(2):
        for pc in range(2):
            v = None
            for rho in range(2):
                at = (pr + rho) * span
                d = dot_nt(deep[at : at + lcells, 256 * pc : 256 * pc + 512], weff[pr, pc, rho])
                v = d if v is None else v + d
            s = v * sigmoid(v)
            for i in range(low):
                r = 2 * i + pr
                here = slice(r * span, (r + 1) * span)
                there = slice(i * span, (i + 1) * span)
                pre_c[pc, here] = v[there]
                act_c[pc, here] = (s[there] + act_a[pc, here].astype(F32)).astype(BF16)

    field = narrow_conv(act_c[0], act_c[1], out_ref[...])
    grad_f = []
    for plane in range(2):
        sig = sigma[plane]
        var = sig * sig + 0.25
        c_out = 0.5 * sig * lax.rsqrt(var)
        den = (0.25 / var) * noisy[plane] + c_out * field[plane]
        for r in range(rows):
            den_ref[r, plane] = den[:, r * span : (r + 1) * span]
        weight = 1.0 + packed_ref[plane, 16:17]
        lam = var / (0.25 * sig * sig)
        loss_grad = 2.0 * scale * weight * lam * (den - residual[plane])
        grad_f.append((c_out * loss_grad).astype(BF16).astype(F32))
    table = taps(*[jnp.where(own, g, 0.0) for g in grad_f])
    grad_ref[AT_LAST : AT_LAST + 72] = dot_nn(unfold_back(table, 0), act_c[0]) + dot_nn(
        unfold_back(table, 1), act_c[1]
    )
    table = taps(*grad_f)
    grad_c = []
    for plane in range(2):
        v = dot_tn(unfold_back(table, plane), out_ref[...])
        back[plane] = v
        pre = pre_c[plane]
        s = sigmoid(pre)
        grad_c.append((v * (s * (1.0 + pre * (1.0 - s)))).astype(BF16).astype(F32))
    store_fine(*grad_c)

    sums = {}
    for pr in range(2):
        for pc in range(2):
            g = jnp.concatenate([grad_c[pc][(2 * i + pr) * span : (2 * i + pr + 1) * span] for i in range(low)], 0)
            g = jnp.where(own_l, g, 0.0).T.astype(BF16)
            for rho in range(2):
                at = (pr + rho) * span
                d = dot_nn(g, deep[at : at + lcells, 256 * pc : 256 * pc + 512])
                for gam in range(2):
                    part = d[:, 256 * gam : 256 * gam + 256]
                    for a in groups[pr][rho]:
                        for b in groups[pc][gam]:
                            for h in range(2):
                                at_up = AT_UP + ((3 * a + b) * 2 + h) * 128
                                piece = part[:, 128 * h : 128 * h + 128]
                                if (a, b) in sums:
                                    piece = grad_ref[at_up : at_up + 128] + piece
                                grad_ref[at_up : at_up + 128] = piece
                            sums[(a, b)] = True

    order = ((1, 1), (0, 1), (1, 0), (0, 0))
    v = None
    for k in range(4):
        pr, rho = ((1, 1), (0, 1), (1, 0), (0, 0))[k]
        x = jnp.concatenate([fine[(2 * i + k) * span : (2 * i + k + 1) * span, :] for i in range(low)], 0)
        w = jnp.concatenate([weff[pr, pc, rho, :, 256 * gam : 256 * gam + 256] for pc, gam in order], 0)
        d = dot_nn(x, w)
        v = d if v is None else v + d
    pre = pre_b[...]
    s = sigmoid(pre)
    grad_b = (v * (s * (1.0 + pre * (1.0 - s)))).astype(BF16).astype(F32)
    store_low(deep, grad_b)
    g = jnp.where(own_l, grad_b, 0.0).T.astype(BF16)
    for a in range(3):
        d = dot_nn(g, pool[a * span : a * span + lcells, :])
        for b in range(3):
            at = (3 * a + b) * 256
            grad_ref[at : at + 256] = d[:, 128 * b : 128 * b + 128]

    v = None
    for a in range(3):
        w = jnp.concatenate([down_ref[a, b] for b in (2, 1, 0)], 0)
        d = dot_nn(deep[(2 - a) * span : (2 - a) * span + lcells, :], w)
        v = d if v is None else v + d
    v = 0.25 * v
    total = None
    for plane in range(2):
        spread = jnp.concatenate([v[(r // 2) * span : (r // 2 + 1) * span] for r in range(rows)], 0)
        pre = pre_a[plane]
        s = sigmoid(pre)
        g = (back[plane] + spread) * (s * (1.0 + pre * (1.0 - s)))
        g = jnp.where(own_f, g, 0.0).astype(BF16)
        d = dot_nn(net[plane], g)
        total = d if total is None else total + d
    grad_ref[AT_IN : AT_IN + 216] = total
    grad_ref[AT_END:] = jnp.zeros((grad_ref.shape[0] - AT_END, 128), F32)


def compute(rows, span, scale, total, args):
    cells = rows * span
    low = rows // 2
    lcells = low * span
    vmem = pl.BlockSpec(memory_space=pltpu.VMEM)
    return pl.pallas_call(
        functools.partial(kernel, rows, span, scale),
        out_shape=(
            jax.ShapeDtypeStruct((rows, 2, 8, span), F32),
            jax.ShapeDtypeStruct((total, 128), F32),
        ),
        in_specs=[vmem] * len(args),
        out_specs=(vmem,) * 2,
        scratch_shapes=[
            pltpu.VMEM((cells + 2 * span, 512), BF16),
            pltpu.VMEM((2, cells, 128), F32),
            pltpu.VMEM((2, cells, 128), BF16),
            pltpu.VMEM((lcells + 2 * span, 384), BF16),
            pltpu.VMEM((lcells, 256), F32),
            pltpu.VMEM((lcells + 2 * span, 768), BF16),
            pltpu.VMEM((2, cells, 128), F32),
            pltpu.VMEM((2, cells, 128), BF16),
            pltpu.VMEM((2, cells, 128), F32),
            pltpu.VMEM((2, 2, 2, 128, 512), BF16),
            pltpu.VMEM((2, 216, cells), BF16),
        ],
        compiler_params=pltpu.CompilerParams(vmem_limit_bytes=48 * 1024 * 1024),
    )(*args)


def ring(axis, step):
    count = lax.axis_size(axis)
    return [(i, (i + step) % count) for i in range(count)]


def widen(x, axis):
    head = x[..., :EDGE]
    tail = x[..., -EDGE:]
    left = lax.ppermute(tail, axis, ring(axis, 1))
    right = lax.ppermute(head, axis, ring(axis, -1))
    return jnp.concatenate([left, x, right], -1)


def planes(x):
    c, r, w = x.shape
    return x.reshape(c, r, w // 2, 2).transpose(3, 0, 1, 2).reshape(2, c, r * (w // 2))


def tall(w, channels):
    w = jnp.pad(w.transpose(0, 1, 3, 2), ((0, 0), (0, 0), (0, channels - w.shape[3]), (0, 0)))
    return w.reshape(9 * channels, w.shape[3])


def flat(w):
    return jnp.pad(w, ((0, 0), (0, 0), (0, 8 - w.shape[2]), (0, 0))).reshape(72, w.shape[3])


def local(
    coarse, target, noise, land_mask, level_index,
    frozen_first, frozen_middle, frozen_last, diffuse_in, diffuse_down, diffuse_up, diffuse_out,
):
    n_lat = lax.axis_size("lat")
    rows = coarse.shape[1]
    strip = coarse.shape[2]
    height, breadth = target.shape[1], target.shape[2]
    sigma = 0.02 * 4000.0 ** (level_index.astype(F32) / (LEVELS - 1))
    sigma = jnp.broadcast_to(sigma[None], (1, height, breadth))
    packed = jnp.concatenate([target, noise, land_mask.astype(F32)[None], sigma], 0)
    packed = widen(packed, "lon")
    windows = jnp.stack([packed[:, :, i * strip : i * strip + strip + 2 * EDGE] for i in range(n_lat)], 0)
    windows = lax.all_to_all(windows, "lat", split_axis=0, concat_axis=0, tiled=True)
    packed = windows.transpose(1, 0, 2, 3).reshape(10, rows, strip + 2 * EDGE)
    pad = jnp.zeros((4, rows, strip + 2 * EDGE), F32)
    packed = planes(jnp.concatenate([packed[:4], pad, packed[4:8], pad, packed[8:], pad, pad[:2]], 0))
    wide = widen(coarse, ("lon", "lat")).astype(F32)
    wide = planes(jnp.pad(wide, ((0, 16 - wide.shape[0]), (0, 0), (0, 0))))
    span = strip // 2 + 2 * HALF
    scale = 1.0 / (target.shape[0] * math.sqrt(height * n_lat * breadth * lax.axis_size("lon")))
    n_pair = lax.axis_size("lon") // 2
    chunk = -(-AT_END // (2 * n_pair * n_lat * 16)) * 16
    total = 2 * n_pair * n_lat * chunk
    den, grads = compute(
        rows, span, scale, total,
        (
            wide, packed, tall(frozen_first, 16), frozen_middle, flat(frozen_last),
            tall(diffuse_in, 24), diffuse_down, diffuse_up, flat(diffuse_out),
        ),
    )
    den, grads = reduce_all(den, grads, n_pair, n_lat, chunk, height)
    den = den[:, :, :, :4, HALF : span - HALF]
    den = den.transpose(3, 1, 0, 4, 2).reshape(4, height, breadth)
    gdown = grads[:AT_UP].reshape(3, 3, 256, 128).astype(F32)
    gup = grads[AT_UP:AT_IN].reshape(3, 3, 2, 128, 128).transpose(0, 1, 3, 2, 4).reshape(3, 3, 128, 256).astype(F32)
    gin = grads[AT_IN:AT_LAST].reshape(3, 3, 24, 128)[:, :, : diffuse_in.shape[3]].transpose(0, 1, 3, 2).astype(F32)
    glast = grads[AT_LAST:AT_END].reshape(3, 3, 8, 128)[:, :, :4].astype(F32)
    return den, gin, gdown, gup, glast


def reduce_kernel(
    n_pair, n_z, chunk, height,
    den_ref, x_ref, den_out, out_ref,
    got1, give2, got2, acc, got3,
    ss1, rs1, ss2, rs2, ss3, rs3, ss4, rs4, ss5, rs5, ss6, rs6, ssd, rsd, own_sem,
):
    lon = lax.axis_index("lon")
    z = lax.axis_index("lat")
    core = lax.rem(lon, 2)
    me = lon // 2
    block = n_z * chunk
    half = n_pair * block
    peer = (me * 2 + 1 - core, z)

    def chip(d):
        return lax.rem(me + d, n_pair)

    def plane(d):
        return lax.rem(z + d, n_z)

    def at_chip(k):
        return (k * 2 + core, z)

    def at_plane(k):
        return (lon, k)

    def rows_at(start, count):
        return pl.ds(pl.multiple_of(start, 16), count)

    def copy(src, dst, send, recv, where):
        return pltpu.make_async_remote_copy(
            src_ref=src, dst_ref=dst, send_sem=send, recv_sem=recv,
            device_id=where, device_id_type=pl.DeviceIdType.MESH,
        )

    barrier = pltpu.get_barrier_semaphore()
    partners = [peer] + [at_chip(chip(d)) for d in range(1, n_pair)] + [at_plane(plane(d)) for d in range(1, n_z)]
    for where in partners:
        pl.semaphore_signal(barrier, inc=1, device_id=where, device_id_type=pl.DeviceIdType.MESH)
    pl.semaphore_wait(barrier, len(partners))

    sent = []

    def start(c):
        c.start()
        sent.append(c)

    order = list(range(1, n_pair)) + [0]
    pieces = []
    for d in order:
        k = chip(d)
        c = copy(
            x_ref.at[rows_at((1 - core) * half + k * block, block)],
            got1.at[rows_at(k * block, block)], ss1.at[d], rs1.at[d], peer,
        )
        start(c)
        pieces.append(c)
    for d in range(1, n_z):
        k = plane(d)
        start(copy(den_ref.at[pl.ds(k * height, height)], den_out.at[z], ssd.at[d], rsd.at[d], at_plane(k)))
    own = pltpu.make_async_copy(den_ref.at[pl.ds(z * height, height)], den_out.at[z], own_sem)
    own.start()
    for d, c in zip(order, pieces):
        c.wait_recv()
        k = chip(d)
        pair = x_ref[rows_at(core * half + k * block, block), :] + got1[rows_at(k * block, block), :]
        if d:
            give2[d] = pair.astype(BF16)
            start(copy(give2.at[d], got2.at[d], ss2.at[d], rs2.at[d], at_chip(k)))
        else:
            acc[...] = pair
    for d in range(1, n_pair):
        copy(give2.at[d], got2.at[d], ss2.at[d], rs2.at[d], at_chip(chip(d))).wait_recv()
    for d in list(range(1, n_z)) + [0]:
        here = rows_at(plane(d) * chunk, chunk)
        s = acc[here, :]
        for e in range(1, n_pair):
            s = s + got2[e, here, :].astype(F32)
        acc[here, :] = s
        if d:
            start(copy(acc.at[here], got3.at[d], ss3.at[d], rs3.at[d], at_plane(plane(d))))
    s = acc[rows_at(z * chunk, chunk), :]
    for d in range(1, n_z):
        copy(acc.at[rows_at(0, chunk)], got3.at[d], ss3.at[d], rs3.at[d], at_plane(plane(d))).wait_recv()
        s = s + got3[d]

    def place(k, p):
        return out_ref.at[rows_at(core * half + k * block + p * chunk, chunk)]

    out_ref[rows_at(core * half + me * block + z * chunk, chunk), :] = s.astype(BF16)
    mine = place(me, z)
    for d in range(1, n_z):
        start(copy(mine, mine, ss4.at[d], rs4.at[d], at_plane(plane(d))))

    def pass_on(d):
        ref = place(me, plane(d))
        for e in range(1, n_pair):
            start(copy(ref, ref, ss5.at[d, e], rs5.at[d, e], at_chip(chip(e))))
        start(copy(ref, ref, ss6.at[d, 0], rs6.at[d, 0], peer))

    def arrived(d):
        for e in range(1, n_pair):
            ref = place(chip(n_pair - e), plane(d))
            copy(ref, ref, ss5.at[d, e], rs5.at[d, e], at_chip(chip(e))).wait_recv()
            start(copy(ref, ref, ss6.at[d, e], rs6.at[d, e], peer))

    pass_on(0)
    for d in range(1, n_z):
        ref = place(me, plane(d))
        copy(ref, ref, ss4.at[n_z - d], rs4.at[n_z - d], at_plane(plane(d))).wait_recv()
        pass_on(d)
        arrived(d - 1)
    arrived(n_z - 1)

    def from_peer(k, p):
        return out_ref.at[rows_at((1 - core) * half + k * block + p * chunk, chunk)]

    for d in range(n_z):
        for e in range(n_pair):
            ref = from_peer(chip(n_pair - e), plane(d))
            copy(ref, ref, ss6.at[d, e], rs6.at[d, e], peer).wait_recv()
    for d in range(1, n_z):
        k = plane(n_z - d)
        copy(den_ref.at[pl.ds(0, height)], den_out.at[k], ssd.at[d], rsd.at[d], at_plane(k)).wait_recv()
    own.wait()
    for c in sent:
        c.wait_send()


def reduce_all(den, grads, n_pair, n_lat, chunk, height):
    block = n_lat * chunk
    vmem = pl.BlockSpec(memory_space=pltpu.VMEM)
    dma = pltpu.SemaphoreType.DMA
    sems = [(n_pair,)] * 4 + [(n_lat,)] * 4 + [(n_lat, n_pair)] * 4 + [(n_lat,)] * 2
    return pl.pallas_call(
        functools.partial(reduce_kernel, n_pair, n_lat, chunk, height),
        out_shape=(
            jax.ShapeDtypeStruct((n_lat, height) + den.shape[1:], F32),
            jax.ShapeDtypeStruct(grads.shape, BF16),
        ),
        in_specs=[vmem] * 2,
        out_specs=(vmem,) * 2,
        scratch_shapes=[
            pltpu.VMEM((n_pair * block, 128), F32),
            pltpu.VMEM((n_pair, block, 128), BF16),
            pltpu.VMEM((n_pair, block, 128), BF16),
            pltpu.VMEM((block, 128), F32),
            pltpu.VMEM((n_lat, chunk, 128), F32),
        ]
        + [dma(s) for s in sems]
        + [dma],
        compiler_params=pltpu.CompilerParams(
            collective_id=1, has_side_effects=True, vmem_limit_bytes=48 * 1024 * 1024
        ),
    )(den, grads)


def solution(mesh):
    return jax.shard_map(
        local,
        mesh=mesh,
        in_specs=(
            P(None, None, ("lon", "lat")),
            P(None, "lat", "lon"),
            P(None, "lat", "lon"),
            P("lat", "lon"),
            P("lat", "lon"),
            P(), P(), P(), P(), P(), P(), P(),
        ),
        out_specs=(P(None, "lat", "lon"), P(), P(), P(), P()),
        check_vma=False,
    )
```

```python
import functools
import math

import jax
import jax.numpy as jnp
from jax import lax
from jax.experimental import pallas as pl
from jax.experimental.pallas import tpu as pltpu
from jax.sharding import PartitionSpec as P

LEVELS = 32
EDGE = 16
HALF = EDGE // 2
AT_UP = 9 * 256
AT_IN = AT_UP + 9 * 256
AT_LAST = AT_IN + 216
AT_END = AT_LAST + 72
F32 = jnp.float32
BF16 = jnp.bfloat16


def dot_nt(x, y):
    return lax.dot_general(x, y, (((1,), (1,)), ((), ())), preferred_element_type=F32)


def dot_tn(x, y):
    return lax.dot_general(x, y, (((0,), (0,)), ((), ())), preferred_element_type=F32)


def dot_nn(x, y):
    return jnp.dot(x, y, preferred_element_type=F32)


def sigmoid(v):
    return 1.0 / (1.0 + jnp.exp(-v))


def roll(x, amount, axis):
    size = x.shape[axis]
    return pltpu.roll(x, amount % size, axis)


def kernel(
    rows, span, scale,
    coarse_ref, packed_ref, first_ref, middle_ref, last_ref, in_ref, down_ref, up_ref, out_ref,
    den_ref, grad_ref,
    fine, pre_a, act_a, pool, pre_b, deep, pre_c, act_c, back, weff, net,
):
    cells = rows * span
    low = rows // 2
    lcells = low * span
    lane = lax.broadcasted_iota(jnp.int32, (1, cells), 1)
    row_of = lane // span
    col_of = lane - row_of * span
    own = (col_of >= HALF) & (col_of < span - HALF)
    col_l = lax.broadcasted_iota(jnp.int32, (lcells, 1), 0) % span
    own_l = (col_l >= HALF) & (col_l < span - HALF)
    col_f = lax.broadcasted_iota(jnp.int32, (cells, 1), 0) % span
    own_f = (col_f >= HALF) & (col_f < span - HALF)

    def row_shift(x, step):
        if step == 0:
            return x
        ok = (row_of + step >= 0) & (row_of + step < rows)
        return jnp.where(ok, roll(x, -step * span, 1), 0.0)

    def col_sources(even, odd):
        return [roll(odd, 1, 1), even, odd, roll(even, -1, 1)]

    def taps(even, odd):
        src = col_sources(even, odd)
        return [[row_shift(s, a - 1) for s in src] for a in range(3)]

    def unfold(table, plane):
        parts = [table[a][plane + b] for a in range(3) for b in range(3)]
        return jnp.concatenate(parts, 0).astype(BF16)

    def unfold_back(table, plane):
        parts = [table[2 - a][plane + 2 - b] for a in range(3) for b in range(3)]
        return jnp.concatenate(parts, 0).astype(BF16)

    def narrow_conv(x_even, x_odd, w):
        ys = (dot_nt(w, x_even), dot_nt(w, x_odd))
        outs = []
        for plane in range(2):
            total = None
            for a in range(3):
                part = None
                for b in range(3):
                    k = plane + b
                    y = ys[(k + 1) % 2][(3 * a + b) * 8 : (3 * a + b) * 8 + 8]
                    if k == 0:
                        y = roll(y, 1, 1)
                    if k == 3:
                        y = roll(y, -1, 1)
                    part = y if part is None else part + y
                part = row_shift(part, a - 1)
                total = part if total is None else total + part
            outs.append(total)
        return outs

    def store_fine(even, odd):
        for k, v in enumerate((roll(odd, 1, 0), even, odd, roll(even, -1, 0))):
            fine[span : span + cells, 128 * k : 128 * k + 128] = v.astype(BF16)

    def store_low(ref, v):
        c = v.shape[1]
        for k, s in enumerate((roll(v, 1, 0), v, roll(v, -1, 0))):
            ref[span : span + lcells, c * k : c * k + c] = s.astype(BF16)

    for ref, count in ((fine, rows), (pool, low), (deep, low)):
        zero = jnp.zeros((span, ref.shape[1]), BF16)
        ref[0:span, :] = zero
        ref[(count + 1) * span : (count + 2) * span, :] = zero

    coarse = (coarse_ref[0], coarse_ref[1])
    table = taps(*coarse)
    first = []
    for plane in range(2):
        v = dot_tn(unfold(table, plane), first_ref[...])
        first.append((v * sigmoid(v)).astype(BF16).astype(F32))
    store_fine(*first)
    second = []
    for plane in range(2):
        v = None
        for a in range(3):
            w = jnp.concatenate([middle_ref[a, b] for b in range(3)], 1)
            d = dot_nt(fine[a * span : a * span + cells, 128 * plane : 128 * plane + 384], w)
            v = d if v is None else v + d
        second.append((v * sigmoid(v)).astype(BF16))
    mean = [m.astype(BF16).astype(F32) for m in narrow_conv(second[0], second[1], last_ref[...])]

    residual, noisy, sigma, mixed = [], [], [], []
    for plane in range(2):
        sig = packed_ref[plane, 17:18]
        res = packed_ref[plane, 0:8] - mean[plane]
        noi = res + sig * packed_ref[plane, 8:16]
        c_in = lax.rsqrt(sig * sig + 0.25)
        scaled = (c_in * noi).astype(BF16).astype(F32)
        mixed.append(jnp.concatenate([mean[plane] + roll(scaled, 4, 0), coarse[plane]], 0))
        residual.append(res)
        noisy.append(noi)
        sigma.append(sig)
    table = taps(*mixed)
    for plane in range(2):
        net[plane] = unfold(table, plane)
        v = dot_tn(net[plane], in_ref[...])
        pre_a[plane] = v
        act_a[plane] = (v * sigmoid(v)).astype(BF16)

    parts = []
    for i in range(low):
        total = None
        for r in (2 * i, 2 * i + 1):
            for plane in range(2):
                v = act_a[plane, r * span : (r + 1) * span].astype(F32)
                total = v if total is None else total + v
        parts.append(0.25 * total)
    store_low(pool, jnp.concatenate(parts, 0).astype(BF16).astype(F32))
    v = None
    for a in range(3):
        w = jnp.concatenate([down_ref[a, b] for b in range(3)], 1)
        d = dot_nt(pool[a * span : a * span + lcells, :], w)
        v = d if v is None else v + d
    pre_b[...] = v
    store_low(deep, (v * sigmoid(v)).astype(BF16).astype(F32))

    groups = (((0,), (1, 2)), ((0, 1), (2,)))
    for pr in range(2):
        for pc in range(2):
            for rho in range(2):
                for gam in range(2):
                    w = None
                    for a in groups[pr][rho]:
                        for b in groups[pc][gam]:
                            u = up_ref[a, b].astype(F32)
                            w = u if w is None else w + u
                    weff[pr, pc, rho, :, 256 * gam : 256 * gam + 256] = w.astype(BF16)
    for pr in range(2):
        for pc in range(2):
            v = None
            for rho in range(2):
                at = (pr + rho) * span
                d = dot_nt(deep[at : at + lcells, 256 * pc : 256 * pc + 512], weff[pr, pc, rho])
                v = d if v is None else v + d
            s = v * sigmoid(v)
            for i in range(low):
                r = 2 * i + pr
                here = slice(r * span, (r + 1) * span)
                there = slice(i * span, (i + 1) * span)
                pre_c[pc, here] = v[there]
                act_c[pc, here] = (s[there] + act_a[pc, here].astype(F32)).astype(BF16)

    field = narrow_conv(act_c[0], act_c[1], out_ref[...])
    grad_f = []
    for plane in range(2):
        sig = sigma[plane]
        var = sig * sig + 0.25
        c_out = 0.5 * sig * lax.rsqrt(var)
        den = (0.25 / var) * noisy[plane] + c_out * field[plane]
        for r in range(rows):
            den_ref[r, plane] = den[:, r * span : (r + 1) * span]
        weight = 1.0 + packed_ref[plane, 16:17]
        lam = var / (0.25 * sig * sig)
        loss_grad = 2.0 * scale * weight * lam * (den - residual[plane])
        grad_f.append((c_out * loss_grad).astype(BF16).astype(F32))
    table = taps(*[jnp.where(own, g, 0.0) for g in grad_f])
    grad_ref[AT_LAST : AT_LAST + 72] = dot_nn(unfold_back(table, 0), act_c[0]) + dot_nn(
        unfold_back(table, 1), act_c[1]
    )
    table = taps(*grad_f)
    grad_c = []
    for plane in range(2):
        v = dot_tn(unfold_back(table, plane), out_ref[...])
        back[plane] = v
        pre = pre_c[plane]
        s = sigmoid(pre)
        grad_c.append((v * (s * (1.0 + pre * (1.0 - s)))).astype(BF16).astype(F32))
    store_fine(*grad_c)

    sums = {}
    for pr in range(2):
        for pc in range(2):
            g = jnp.concatenate([grad_c[pc][(2 * i + pr) * span : (2 * i + pr + 1) * span] for i in range(low)], 0)
            g = jnp.where(own_l, g, 0.0).T.astype(BF16)
            for rho in range(2):
                at = (pr + rho) * span
                d = dot_nn(g, deep[at : at + lcells, 256 * pc : 256 * pc + 512])
                for gam in range(2):
                    part = d[:, 256 * gam : 256 * gam + 256]
                    for a in groups[pr][rho]:
                        for b in groups[pc][gam]:
                            for h in range(2):
                                at_up = AT_UP + ((3 * a + b) * 2 + h) * 128
                                piece = part[:, 128 * h : 128 * h + 128]
                                if (a, b) in sums:
                                    piece = grad_ref[at_up : at_up + 128] + piece
                                grad_ref[at_up : at_up + 128] = piece
                            sums[(a, b)] = True

    order = ((1, 1), (0, 1), (1, 0), (0, 0))
    v = None
    for k in range(4):
        pr, rho = ((1, 1), (0, 1), (1, 0), (0, 0))[k]
        x = jnp.concatenate([fine[(2 * i + k) * span : (2 * i + k + 1) * span, :] for i in range(low)], 0)
        w = jnp.concatenate([weff[pr, pc, rho, :, 256 * gam : 256 * gam + 256] for pc, gam in order], 0)
        d = dot_nn(x, w)
        v = d if v is None else v + d
    pre = pre_b[...]
    s = sigmoid(pre)
    grad_b = (v * (s * (1.0 + pre * (1.0 - s)))).astype(BF16).astype(F32)
    store_low(deep, grad_b)
    g = jnp.where(own_l, grad_b, 0.0).T.astype(BF16)
    for a in range(3):
        d = dot_nn(g, pool[a * span : a * span + lcells, :])
        for b in range(3):
            at = (3 * a + b) * 256
            grad_ref[at : at + 256] = d[:, 128 * b : 128 * b + 128]

    v = None
    for a in range(3):
        w = jnp.concatenate([down_ref[a, b] for b in (2, 1, 0)], 0)
        d = dot_nn(deep[(2 - a) * span : (2 - a) * span + lcells, :], w)
        v = d if v is None else v + d
    v = 0.25 * v
    total = None
    for plane in range(2):
        spread = jnp.concatenate([v[(r // 2) * span : (r // 2 + 1) * span] for r in range(rows)], 0)
        pre = pre_a[plane]
        s = sigmoid(pre)
        g = (back[plane] + spread) * (s * (1.0 + pre * (1.0 - s)))
        g = jnp.where(own_f, g, 0.0).astype(BF16)
        d = dot_nn(net[plane], g)
        total = d if total is None else total + d
    grad_ref[AT_IN : AT_IN + 216] = total
    grad_ref[AT_END:] = jnp.zeros((grad_ref.shape[0] - AT_END, 128), F32)


def compute(rows, span, scale, total, args):
    cells = rows * span
    low = rows // 2
    lcells = low * span
    vmem = pl.BlockSpec(memory_space=pltpu.VMEM)
    return pl.pallas_call(
        functools.partial(kernel, rows, span, scale),
        out_shape=(
            jax.ShapeDtypeStruct((rows, 2, 8, span), F32),
            jax.ShapeDtypeStruct((total, 128), F32),
        ),
        in_specs=[vmem] * len(args),
        out_specs=(vmem,) * 2,
        scratch_shapes=[
            pltpu.VMEM((cells + 2 * span, 512), BF16),
            pltpu.VMEM((2, cells, 128), F32),
            pltpu.VMEM((2, cells, 128), BF16),
            pltpu.VMEM((lcells + 2 * span, 384), BF16),
            pltpu.VMEM((lcells, 256), F32),
            pltpu.VMEM((lcells + 2 * span, 768), BF16),
            pltpu.VMEM((2, cells, 128), F32),
            pltpu.VMEM((2, cells, 128), BF16),
            pltpu.VMEM((2, cells, 128), F32),
            pltpu.VMEM((2, 2, 2, 128, 512), BF16),
            pltpu.VMEM((2, 216, cells), BF16),
        ],
        compiler_params=pltpu.CompilerParams(vmem_limit_bytes=48 * 1024 * 1024),
    )(*args)


def ring(axis, step):
    count = lax.axis_size(axis)
    return [(i, (i + step) % count) for i in range(count)]


def widen(x, axis):
    head = x[..., :EDGE]
    tail = x[..., -EDGE:]
    left = lax.ppermute(tail, axis, ring(axis, 1))
    right = lax.ppermute(head, axis, ring(axis, -1))
    return jnp.concatenate([left, x, right], -1)


def planes(x):
    c, r, w = x.shape
    return x.reshape(c, r, w // 2, 2).transpose(3, 0, 1, 2).reshape(2, c, r * (w // 2))


def tall(w, channels):
    w = jnp.pad(w.transpose(0, 1, 3, 2), ((0, 0), (0, 0), (0, channels - w.shape[3]), (0, 0)))
    return w.reshape(9 * channels, w.shape[3])


def flat(w):
    return jnp.pad(w, ((0, 0), (0, 0), (0, 8 - w.shape[2]), (0, 0))).reshape(72, w.shape[3])


def local(
    coarse, target, noise, land_mask, level_index,
    frozen_first, frozen_middle, frozen_last, diffuse_in, diffuse_down, diffuse_up, diffuse_out,
):
    n_lat = lax.axis_size("lat")
    rows = coarse.shape[1]
    strip = coarse.shape[2]
    height, breadth = target.shape[1], target.shape[2]
    sigma = 0.02 * 4000.0 ** (level_index.astype(F32) / (LEVELS - 1))
    sigma = jnp.broadcast_to(sigma[None], (1, height, breadth))
    packed = jnp.concatenate([target, noise, land_mask.astype(F32)[None], sigma], 0)
    packed = widen(packed, "lon")
    windows = jnp.stack([packed[:, :, i * strip : i * strip + strip + 2 * EDGE] for i in range(n_lat)], 0)
    windows = lax.all_to_all(windows, "lat", split_axis=0, concat_axis=0, tiled=True)
    packed = windows.transpose(1, 0, 2, 3).reshape(10, rows, strip + 2 * EDGE)
    pad = jnp.zeros((4, rows, strip + 2 * EDGE), F32)
    packed = planes(jnp.concatenate([packed[:4], pad, packed[4:8], pad, packed[8:], pad, pad[:2]], 0))
    wide = widen(coarse, ("lon", "lat")).astype(F32)
    wide = planes(jnp.pad(wide, ((0, 16 - wide.shape[0]), (0, 0), (0, 0))))
    span = strip // 2 + 2 * HALF
    scale = 1.0 / (target.shape[0] * math.sqrt(height * n_lat * breadth * lax.axis_size("lon")))
    n_pair = lax.axis_size("lon") // 2
    chunk = -(-AT_END // (2 * n_pair * n_lat * 16)) * 16
    total = 2 * n_pair * n_lat * chunk
    den, grads = compute(
        rows, span, scale, total,
        (
            wide, packed, tall(frozen_first, 16), frozen_middle, flat(frozen_last),
            tall(diffuse_in, 24), diffuse_down, diffuse_up, flat(diffuse_out),
        ),
    )
    den, grads = reduce_all(den, grads, n_pair, n_lat, chunk, height)
    den = den[:, :, :, :4, HALF : span - HALF]
    den = den.transpose(3, 1, 0, 4, 2).reshape(4, height, breadth)
    gdown = grads[:AT_UP].reshape(3, 3, 256, 128).astype(F32)
    gup = grads[AT_UP:AT_IN].reshape(3, 3, 2, 128, 128).transpose(0, 1, 3, 2, 4).reshape(3, 3, 128, 256).astype(F32)
    gin = grads[AT_IN:AT_LAST].reshape(3, 3, 24, 128)[:, :, : diffuse_in.shape[3]].transpose(0, 1, 3, 2).astype(F32)
    glast = grads[AT_LAST:AT_END].reshape(3, 3, 8, 128)[:, :, :4].astype(F32)
    return den, gin, gdown, gup, glast


def reduce_kernel(
    n_pair, n_z, chunk, height,
    den_ref, x_ref, den_out, out_ref,
    got1, give2, got2, acc, give3, got3,
    ss1, rs1, ss2, rs2, ss3, rs3, ss4, rs4, ss5, rs5, ss6, rs6, ssd, rsd, own_sem,
):
    lon = lax.axis_index("lon")
    z = lax.axis_index("lat")
    core = lax.rem(lon, 2)
    me = lon // 2
    block = n_z * chunk
    half = n_pair * block
    peer = (me * 2 + 1 - core, z)

    def chip(d):
        return lax.rem(me + d, n_pair)

    def plane(d):
        return lax.rem(z + d, n_z)

    def at_chip(k):
        return (k * 2 + core, z)

    def at_plane(k):
        return (lon, k)

    def rows_at(start, count):
        return pl.ds(pl.multiple_of(start, 16), count)

    def copy(src, dst, send, recv, where):
        return pltpu.make_async_remote_copy(
            src_ref=src, dst_ref=dst, send_sem=send, recv_sem=recv,
            device_id=where, device_id_type=pl.DeviceIdType.MESH,
        )

    barrier = pltpu.get_barrier_semaphore()
    partners = [peer] + [at_chip(chip(d)) for d in range(1, n_pair)] + [at_plane(plane(d)) for d in range(1, n_z)]
    for where in partners:
        pl.semaphore_signal(barrier, inc=1, device_id=where, device_id_type=pl.DeviceIdType.MESH)
    pl.semaphore_wait(barrier, len(partners))

    sent = []

    def start(c):
        c.start()
        sent.append(c)

    chips = list(range(1, n_pair)) + [0]
    planes_on = list(range(1, n_z)) + [0]
    pieces = {}
    for d in planes_on:
        for e in chips:
            at = chip(e) * block + plane(d) * chunk
            c = copy(
                x_ref.at[rows_at((1 - core) * half + at, chunk)],
                got1.at[rows_at(at, chunk)], ss1.at[d, e], rs1.at[d, e], peer,
            )
            start(c)
            pieces[d, e] = c
    for d in range(1, n_z):
        k = plane(d)
        start(copy(den_ref.at[pl.ds(k * height, height)], den_out.at[z], ssd.at[d], rsd.at[d], at_plane(k)))
    own = pltpu.make_async_copy(den_ref.at[pl.ds(z * height, height)], den_out.at[z], own_sem)
    own.start()

    def add_pair(d):
        for e in chips:
            pieces[d, e].wait_recv()
            at = chip(e) * block + plane(d) * chunk
            pair = x_ref[rows_at(core * half + at, chunk), :] + got1[rows_at(at, chunk), :]
            if e:
                give2[d, e] = pair.astype(BF16)
                start(copy(give2.at[d, e], got2.at[d, e], ss2.at[d, e], rs2.at[d, e], at_chip(chip(e))))
            else:
                acc[d] = pair

    def add_plane(d):
        for e in range(1, n_pair):
            copy(give2.at[d, e], got2.at[d, e], ss2.at[d, e], rs2.at[d, e], at_chip(chip(e))).wait_recv()
        s = acc[d]
        for e in range(1, n_pair):
            s = s + got2[d, e].astype(F32)
        if d:
            give3[d] = s.astype(BF16)
            start(copy(give3.at[d], got3.at[d], ss3.at[d], rs3.at[d], at_plane(plane(d))))
        return s

    for n, d in enumerate(planes_on):
        add_pair(d)
        if n:
            add_plane(planes_on[n - 1])
    s = add_plane(0)
    for d in range(1, n_z):
        copy(give3.at[d], got3.at[d], ss3.at[d], rs3.at[d], at_plane(plane(d))).wait_recv()
        s = s + got3[d].astype(F32)

    def place(k, p):
        return out_ref.at[rows_at(core * half + k * block + p * chunk, chunk)]

    out_ref[rows_at(core * half + me * block + z * chunk, chunk), :] = s.astype(BF16)
    mine = place(me, z)
    for d in range(1, n_z):
        start(copy(mine, mine, ss4.at[d], rs4.at[d], at_plane(plane(d))))

    def pass_on(d):
        ref = place(me, plane(d))
        for e in range(1, n_pair):
            start(copy(ref, ref, ss5.at[d, e], rs5.at[d, e], at_chip(chip(e))))
        start(copy(ref, ref, ss6.at[d, 0], rs6.at[d, 0], peer))

    def arrived(d):
        for e in range(1, n_pair):
            ref = place(chip(n_pair - e), plane(d))
            copy(ref, ref, ss5.at[d, e], rs5.at[d, e], at_chip(chip(e))).wait_recv()
            start(copy(ref, ref, ss6.at[d, e], rs6.at[d, e], peer))

    pass_on(0)
    for d in range(1, n_z):
        ref = place(me, plane(d))
        copy(ref, ref, ss4.at[n_z - d], rs4.at[n_z - d], at_plane(plane(d))).wait_recv()
        pass_on(d)
        arrived(d - 1)
    arrived(n_z - 1)

    def from_peer(k, p):
        return out_ref.at[rows_at((1 - core) * half + k * block + p * chunk, chunk)]

    for d in range(n_z):
        for e in range(n_pair):
            ref = from_peer(chip(n_pair - e), plane(d))
            copy(ref, ref, ss6.at[d, e], rs6.at[d, e], peer).wait_recv()
    for d in range(1, n_z):
        k = plane(n_z - d)
        copy(den_ref.at[pl.ds(0, height)], den_out.at[k], ssd.at[d], rsd.at[d], at_plane(k)).wait_recv()
    own.wait()
    for c in sent:
        c.wait_send()


def reduce_all(den, grads, n_pair, n_lat, chunk, height):
    block = n_lat * chunk
    vmem = pl.BlockSpec(memory_space=pltpu.VMEM)
    dma = pltpu.SemaphoreType.DMA
    sems = [(n_lat, n_pair)] * 4 + [(n_lat,)] * 4 + [(n_lat, n_pair)] * 4 + [(n_lat,)] * 2
    return pl.pallas_call(
        functools.partial(reduce_kernel, n_pair, n_lat, chunk, height),
        out_shape=(
            jax.ShapeDtypeStruct((n_lat, height) + den.shape[1:], F32),
            jax.ShapeDtypeStruct(grads.shape, BF16),
        ),
        in_specs=[vmem] * 2,
        out_specs=(vmem,) * 2,
        scratch_shapes=[
            pltpu.VMEM((n_pair * block, 128), F32),
            pltpu.VMEM((n_lat, n_pair, chunk, 128), BF16),
            pltpu.VMEM((n_lat, n_pair, chunk, 128), BF16),
            pltpu.VMEM((n_lat, chunk, 128), F32),
            pltpu.VMEM((n_lat, chunk, 128), BF16),
            pltpu.VMEM((n_lat, chunk, 128), BF16),
        ]
        + [dma(s) for s in sems]
        + [dma],
        compiler_params=pltpu.CompilerParams(
            collective_id=1, has_side_effects=True, vmem_limit_bytes=48 * 1024 * 1024
        ),
    )(den, grads)


def solution(mesh):
    return jax.shard_map(
        local,
        mesh=mesh,
        in_specs=(
            P(None, None, ("lon", "lat")),
            P(None, "lat", "lon"),
            P(None, "lat", "lon"),
            P("lat", "lon"),
            P("lat", "lon"),
            P(), P(), P(), P(), P(), P(), P(),
        ),
        out_specs=(P(None, "lat", "lon"), P(), P(), P(), P()),
        check_vma=False,
    )
```

```python
import functools
import math

import jax
import jax.numpy as jnp
from jax import lax
from jax.experimental import pallas as pl
from jax.experimental.pallas import tpu as pltpu
from jax.sharding import PartitionSpec as P

LEVELS = 32
EDGE = 16
HALF = EDGE // 2
AT_UP = 9 * 256
AT_IN = AT_UP + 9 * 256
AT_LAST = AT_IN + 216
AT_END = AT_LAST + 72
GROUPS = (((0,), (1, 2)), ((0, 1), (2,)))
F32 = jnp.float32
BF16 = jnp.bfloat16


def dot_nt(x, y):
    return lax.dot_general(x, y, (((1,), (1,)), ((), ())), preferred_element_type=F32)


def dot_tn(x, y):
    return lax.dot_general(x, y, (((0,), (0,)), ((), ())), preferred_element_type=F32)


def dot_nn(x, y):
    return jnp.dot(x, y, preferred_element_type=F32)


def sigmoid(v):
    return 1.0 / (1.0 + jnp.exp(-v))


def roll(x, amount, axis):
    size = x.shape[axis]
    return pltpu.roll(x, amount % size, axis)


def kernel(
    rows, span, scale,
    coarse_ref, packed_ref, first_ref, last_ref, in_ref, out_ref, weff, middle_ref, down_ref,
    den_ref, grad_ref,
    fine, pre_a, act_a, pool, pre_b, deep, pre_c, act_c, back, net,
):
    cells = rows * span
    low = rows // 2
    lcells = low * span
    lane = lax.broadcasted_iota(jnp.int32, (1, cells), 1)
    row_of = lane // span
    col_of = lane - row_of * span
    own = (col_of >= HALF) & (col_of < span - HALF)
    col_l = lax.broadcasted_iota(jnp.int32, (lcells, 1), 0) % span
    own_l = (col_l >= HALF) & (col_l < span - HALF)
    col_f = lax.broadcasted_iota(jnp.int32, (cells, 1), 0) % span
    own_f = (col_f >= HALF) & (col_f < span - HALF)

    def row_shift(x, step):
        if step == 0:
            return x
        ok = (row_of + step >= 0) & (row_of + step < rows)
        return jnp.where(ok, roll(x, -step * span, 1), 0.0)

    def col_sources(even, odd):
        return [roll(odd, 1, 1), even, odd, roll(even, -1, 1)]

    def taps(even, odd):
        src = col_sources(even, odd)
        return [[row_shift(s, a - 1) for s in src] for a in range(3)]

    def unfold(table, plane):
        parts = [table[a][plane + b] for a in range(3) for b in range(3)]
        return jnp.concatenate(parts, 0).astype(BF16)

    def unfold_back(table, plane):
        parts = [table[2 - a][plane + 2 - b] for a in range(3) for b in range(3)]
        return jnp.concatenate(parts, 0).astype(BF16)

    def narrow_conv(x_even, x_odd, w):
        ys = (dot_nt(w, x_even), dot_nt(w, x_odd))
        outs = []
        for plane in range(2):
            total = None
            for a in range(3):
                part = None
                for b in range(3):
                    k = plane + b
                    y = ys[(k + 1) % 2][(3 * a + b) * 8 : (3 * a + b) * 8 + 8]
                    if k == 0:
                        y = roll(y, 1, 1)
                    if k == 3:
                        y = roll(y, -1, 1)
                    part = y if part is None else part + y
                part = row_shift(part, a - 1)
                total = part if total is None else total + part
            outs.append(total)
        return outs

    def store_fine(even, odd):
        for k, v in enumerate((roll(odd, 1, 0), even, odd, roll(even, -1, 0))):
            fine[span : span + cells, 128 * k : 128 * k + 128] = v.astype(BF16)

    def store_low(ref, v):
        c = v.shape[1]
        for k, s in enumerate((roll(v, 1, 0), v, roll(v, -1, 0))):
            ref[span : span + lcells, c * k : c * k + c] = s.astype(BF16)

    for ref, count in ((fine, rows), (pool, low), (deep, low)):
        zero = jnp.zeros((span, ref.shape[1]), BF16)
        ref[0:span, :] = zero
        ref[(count + 1) * span : (count + 2) * span, :] = zero

    coarse = (coarse_ref[0], coarse_ref[1])
    table = taps(*coarse)
    first = []
    for plane in range(2):
        v = dot_tn(unfold(table, plane), first_ref[...])
        first.append((v * sigmoid(v)).astype(BF16).astype(F32))
    store_fine(*first)
    second = []
    for plane in range(2):
        v = None
        for a in range(3):
            w = jnp.concatenate([middle_ref[a, b] for b in range(3)], 1)
            d = dot_nt(fine[a * span : a * span + cells, 128 * plane : 128 * plane + 384], w)
            v = d if v is None else v + d
        second.append((v * sigmoid(v)).astype(BF16))
    mean = [m.astype(BF16).astype(F32) for m in narrow_conv(second[0], second[1], last_ref[...])]

    residual, noisy, sigma, mixed = [], [], [], []
    for plane in range(2):
        sig = packed_ref[plane, 17:18]
        res = packed_ref[plane, 0:8] - mean[plane]
        noi = res + sig * packed_ref[plane, 8:16]
        c_in = lax.rsqrt(sig * sig + 0.25)
        scaled = (c_in * noi).astype(BF16).astype(F32)
        mixed.append(jnp.concatenate([mean[plane] + roll(scaled, 4, 0), coarse[plane]], 0))
        residual.append(res)
        noisy.append(noi)
        sigma.append(sig)
    table = taps(*mixed)
    for plane in range(2):
        net[plane] = unfold(table, plane)
        v = dot_tn(net[plane], in_ref[...])
        pre_a[plane] = v
        act_a[plane] = (v * sigmoid(v)).astype(BF16)

    parts = []
    for i in range(low):
        total = None
        for r in (2 * i, 2 * i + 1):
            for plane in range(2):
                v = act_a[plane, r * span : (r + 1) * span].astype(F32)
                total = v if total is None else total + v
        parts.append(0.25 * total)
    store_low(pool, jnp.concatenate(parts, 0).astype(BF16).astype(F32))
    v = None
    for a in range(3):
        w = jnp.concatenate([down_ref[a, b] for b in range(3)], 1)
        d = dot_nt(pool[a * span : a * span + lcells, :], w)
        v = d if v is None else v + d
    pre_b[...] = v
    store_low(deep, (v * sigmoid(v)).astype(BF16).astype(F32))

    for pr in range(2):
        for pc in range(2):
            v = None
            for rho in range(2):
                at = (pr + rho) * span
                d = dot_nt(deep[at : at + lcells, 256 * pc : 256 * pc + 512], weff[pr, pc, rho])
                v = d if v is None else v + d
            s = v * sigmoid(v)
            for i in range(low):
                r = 2 * i + pr
                here = slice(r * span, (r + 1) * span)
                there = slice(i * span, (i + 1) * span)
                pre_c[pc, here] = v[there]
                act_c[pc, here] = (s[there] + act_a[pc, here].astype(F32)).astype(BF16)

    field = narrow_conv(act_c[0], act_c[1], out_ref[...])
    grad_f = []
    for plane in range(2):
        sig = sigma[plane]
        var = sig * sig + 0.25
        c_out = 0.5 * sig * lax.rsqrt(var)
        den = (0.25 / var) * noisy[plane] + c_out * field[plane]
        for r in range(rows):
            den_ref[r, plane] = den[:, r * span : (r + 1) * span]
        weight = 1.0 + packed_ref[plane, 16:17]
        lam = var / (0.25 * sig * sig)
        loss_grad = 2.0 * scale * weight * lam * (den - residual[plane])
        grad_f.append((c_out * loss_grad).astype(BF16).astype(F32))
    table = taps(*[jnp.where(own, g, 0.0) for g in grad_f])
    grad_ref[AT_LAST : AT_LAST + 72] = dot_nn(unfold_back(table, 0), act_c[0]) + dot_nn(
        unfold_back(table, 1), act_c[1]
    )
    table = taps(*grad_f)
    grad_c = []
    for plane in range(2):
        v = dot_tn(unfold_back(table, plane), out_ref[...])
        back[plane] = v
        pre = pre_c[plane]
        s = sigmoid(pre)
        grad_c.append((v * (s * (1.0 + pre * (1.0 - s)))).astype(BF16).astype(F32))
    store_fine(*grad_c)

    sums = {}
    for pr in range(2):
        for pc in range(2):
            g = jnp.concatenate([grad_c[pc][(2 * i + pr) * span : (2 * i + pr + 1) * span] for i in range(low)], 0)
            g = jnp.where(own_l, g, 0.0).T.astype(BF16)
            for rho in range(2):
                at = (pr + rho) * span
                d = dot_nn(g, deep[at : at + lcells, 256 * pc : 256 * pc + 512])
                for gam in range(2):
                    part = d[:, 256 * gam : 256 * gam + 256]
                    for a in GROUPS[pr][rho]:
                        for b in GROUPS[pc][gam]:
                            for h in range(2):
                                at_up = AT_UP + ((3 * a + b) * 2 + h) * 128
                                piece = part[:, 128 * h : 128 * h + 128]
                                if (a, b) in sums:
                                    piece = grad_ref[at_up : at_up + 128] + piece
                                grad_ref[at_up : at_up + 128] = piece
                            sums[(a, b)] = True

    order = ((1, 1), (0, 1), (1, 0), (0, 0))
    v = None
    for k in range(4):
        pr, rho = ((1, 1), (0, 1), (1, 0), (0, 0))[k]
        x = jnp.concatenate([fine[(2 * i + k) * span : (2 * i + k + 1) * span, :] for i in range(low)], 0)
        w = jnp.concatenate([weff[pr, pc, rho, :, 256 * gam : 256 * gam + 256] for pc, gam in order], 0)
        d = dot_nn(x, w)
        v = d if v is None else v + d
    pre = pre_b[...]
    s = sigmoid(pre)
    grad_b = (v * (s * (1.0 + pre * (1.0 - s)))).astype(BF16).astype(F32)
    store_low(deep, grad_b)
    g = jnp.where(own_l, grad_b, 0.0).T.astype(BF16)
    for a in range(3):
        d = dot_nn(g, pool[a * span : a * span + lcells, :])
        for b in range(3):
            at = (3 * a + b) * 256
            grad_ref[at : at + 256] = d[:, 128 * b : 128 * b + 128]

    v = None
    for a in range(3):
        w = jnp.concatenate([down_ref[a, b] for b in (2, 1, 0)], 0)
        d = dot_nn(deep[(2 - a) * span : (2 - a) * span + lcells, :], w)
        v = d if v is None else v + d
    v = 0.25 * v
    total = None
    for plane in range(2):
        spread = jnp.concatenate([v[(r // 2) * span : (r // 2 + 1) * span] for r in range(rows)], 0)
        pre = pre_a[plane]
        s = sigmoid(pre)
        g = (back[plane] + spread) * (s * (1.0 + pre * (1.0 - s)))
        g = jnp.where(own_f, g, 0.0).astype(BF16)
        d = dot_nn(net[plane], g)
        total = d if total is None else total + d
    grad_ref[AT_IN : AT_IN + 216] = total
    grad_ref[AT_END:] = jnp.zeros((grad_ref.shape[0] - AT_END, 128), F32)


def compute(rows, span, scale, total, args):
    cells = rows * span
    low = rows // 2
    lcells = low * span
    vmem = pl.BlockSpec(memory_space=pltpu.VMEM)
    return pl.pallas_call(
        functools.partial(kernel, rows, span, scale),
        out_shape=(
            jax.ShapeDtypeStruct((rows, 2, 8, span), F32),
            jax.ShapeDtypeStruct((total, 128), F32),
        ),
        in_specs=[vmem] * len(args),
        out_specs=(vmem,) * 2,
        scratch_shapes=[
            pltpu.VMEM((cells + 2 * span, 512), BF16),
            pltpu.VMEM((2, cells, 128), F32),
            pltpu.VMEM((2, cells, 128), BF16),
            pltpu.VMEM((lcells + 2 * span, 384), BF16),
            pltpu.VMEM((lcells, 256), F32),
            pltpu.VMEM((lcells + 2 * span, 768), BF16),
            pltpu.VMEM((2, cells, 128), F32),
            pltpu.VMEM((2, cells, 128), BF16),
            pltpu.VMEM((2, cells, 128), F32),
            pltpu.VMEM((2, 216, cells), BF16),
        ],
        compiler_params=pltpu.CompilerParams(vmem_limit_bytes=48 * 1024 * 1024),
    )(*args)


def exchange_kernel(
    n_z, n_lon, strip, height,
    coarse_ref, target_ref, noise_ref, mask_ref, level_ref,
    first_ref, last_ref, in_ref, up_ref, out_ref,
    coarse_out, packed_out, wfirst, wlast, win, wout, weff,
    wide, tile, got, ss_c, rs_c, ss_t, rs_t, ss_z, rs_z, own_sem,
):
    lon = lax.axis_index("lon")
    z = lax.axis_index("lat")
    rows = n_z * height
    span = strip // 2 + 2 * HALF
    breadth = n_z * strip
    strips = n_lon * n_z
    mine = lon * n_z + z

    def of_strip(s):
        return (s // n_z, lax.rem(s, n_z))

    def of_lon(q):
        return (lax.rem(q + n_lon, n_lon), z)

    def plane(d):
        return lax.rem(z + d, n_z)

    def at_plane(k):
        return (lon, k)

    next_strip = of_strip(lax.rem(mine + 1, strips))
    last_strip = of_strip(lax.rem(mine + strips - 1, strips))
    next_lon, last_lon = of_lon(lon + 1), of_lon(lon - 1)

    def copy(src, dst, send, recv, where):
        return pltpu.make_async_remote_copy(
            src_ref=src, dst_ref=dst, send_sem=send, recv_sem=recv,
            device_id=where, device_id_type=pl.DeviceIdType.MESH,
        )

    barrier = pltpu.get_barrier_semaphore()
    partners = [next_strip, last_strip, next_lon, last_lon] + [at_plane(plane(d)) for d in range(1, n_z)]
    for where in partners:
        pl.semaphore_signal(barrier, inc=1, device_id=where, device_id_type=pl.DeviceIdType.MESH)

    level = level_ref[...].astype(F32)
    sigma = 0.02 * jnp.exp(level * (math.log(4000.0) / (LEVELS - 1)))
    body = slice(128, 128 + breadth)
    for c in range(4):
        for r in range(height):
            tile[c * height + r : c * height + r + 1, body] = target_ref[c, r : r + 1, :]
            tile[(4 + c) * height + r : (4 + c) * height + r + 1, body] = noise_ref[c, r : r + 1, :]
    tile[8 * height : 9 * height, body] = mask_ref[...].astype(F32)
    tile[9 * height : 10 * height, body] = jnp.broadcast_to(sigma, (height, breadth))
    for c in range(coarse_ref.shape[0]):
        wide[c * rows : (c + 1) * rows, 128 : 128 + strip] = coarse_ref[c].astype(F32)
    pl.semaphore_wait(barrier, len(partners))

    sent = []

    def start(c):
        c.start()
        sent.append(c)
        return c

    right_t = start(copy(tile.at[:, pl.ds(breadth, 128)], tile.at[:, pl.ds(0, 128)], ss_t.at[0], rs_t.at[0], next_lon))
    left_t = start(copy(tile.at[:, pl.ds(128, 128)], tile.at[:, pl.ds(breadth + 128, 128)], ss_t.at[1], rs_t.at[1], last_lon))
    right_c = start(copy(wide.at[:, pl.ds(strip, 128)], wide.at[:, pl.ds(0, 128)], ss_c.at[0], rs_c.at[0], next_strip))
    left_c = start(copy(wide.at[:, pl.ds(128, 128)], wide.at[:, pl.ds(strip + 128, 128)], ss_c.at[1], rs_c.at[1], last_strip))

    def tall(ref, channels):
        parts = []
        for a in range(3):
            for b in range(3):
                t = ref[a, b].astype(F32).T
                parts.append(t)
                if channels > t.shape[0]:
                    parts.append(jnp.zeros((channels - t.shape[0], t.shape[1]), F32))
        return jnp.concatenate(parts, 0).astype(BF16)

    def flat(ref):
        parts = []
        for a in range(3):
            for b in range(3):
                t = ref[a, b].astype(F32)
                parts += [t, jnp.zeros((8 - t.shape[0], t.shape[1]), F32)]
        return jnp.concatenate(parts, 0).astype(BF16)

    wfirst[...] = tall(first_ref, 16)
    right_t.wait_recv()
    left_t.wait_recv()

    def window(k):
        return tile.at[:, pl.ds(pl.multiple_of(k * strip, 128), strip + 256)]

    for d in range(1, n_z):
        start(copy(window(plane(d)), got.at[z], ss_z.at[d], rs_z.at[d], at_plane(plane(d))))
    own = pltpu.make_async_copy(window(z), got.at[z], own_sem)
    own.start()

    win[...] = tall(in_ref, 24)
    wlast[...] = flat(last_ref)
    wout[...] = flat(out_ref)
    for pr in range(2):
        for pc in range(2):
            for rho in range(2):
                for gam in range(2):
                    w = None
                    for a in GROUPS[pr][rho]:
                        for b in GROUPS[pc][gam]:
                            u = up_ref[a, b].astype(F32)
                            w = u if w is None else w + u
                    weff[pr, pc, rho, :, 256 * gam : 256 * gam + 256] = w.astype(BF16)

    shape = (strip + 256, 2 * span)
    source = lax.broadcasted_iota(jnp.int32, shape, 0)
    slot = lax.broadcasted_iota(jnp.int32, shape, 1)
    parity = (slot >= span).astype(jnp.int32)
    wanted = 128 - EDGE + 2 * (slot - parity * span) + parity
    pick = (source == wanted).astype(F32)

    right_c.wait_recv()
    left_c.wait_recv()
    split = dot_nn(wide[...].astype(BF16), pick.astype(BF16)).reshape(coarse_ref.shape[0], rows, 2 * span)
    coarse_out[...] = jnp.zeros(coarse_out.shape, F32)
    for r in range(rows):
        for p in range(2):
            part = split[:, r, p * span : (p + 1) * span]
            coarse_out[p, 0 : coarse_ref.shape[0], r * span : (r + 1) * span] = part
    for d in range(1, n_z):
        k = plane(n_z - d)
        copy(window(k), got.at[k], ss_z.at[d], rs_z.at[d], at_plane(k)).wait_recv()
    own.wait()
    packed_out[...] = jnp.zeros(packed_out.shape, F32)
    fields = got[...].reshape(n_z * 10 * height, strip + 256)
    total, rest = None, fields
    for _ in range(3):
        term = rest.astype(BF16)
        rest = rest - term.astype(F32)
        part = dot_nn(term, pick.astype(BF16))
        total = part if total is None else total + part
    total = total.reshape(n_z, 10 * height, 2 * span)
    for k in range(n_z):
        for r in range(height):
            here = slice((k * height + r) * span, (k * height + r + 1) * span)
            for p in range(2):
                cut = slice(p * span, (p + 1) * span)
                for c in range(4):
                    packed_out[p, c : c + 1, here] = total[k, c * height + r : c * height + r + 1, cut]
                    packed_out[p, 8 + c : 9 + c, here] = total[k, (4 + c) * height + r : (4 + c) * height + r + 1, cut]
                packed_out[p, 16:17, here] = total[k, 8 * height + r : 8 * height + r + 1, cut]
                packed_out[p, 17:18, here] = total[k, 9 * height + r : 9 * height + r + 1, cut]
    for c in sent:
        c.wait_send()


def exchange(n_z, n_lon, args):
    coarse, target = args[0], args[1]
    channels, rows, strip = coarse.shape
    height = target.shape[1]
    cells = rows * (strip // 2 + 2 * HALF)
    vmem = pl.BlockSpec(memory_space=pltpu.VMEM)
    dma = pltpu.SemaphoreType.DMA
    return pl.pallas_call(
        functools.partial(exchange_kernel, n_z, n_lon, strip, height),
        out_shape=(
            jax.ShapeDtypeStruct((2, 16, cells), F32),
            jax.ShapeDtypeStruct((2, 24, cells), F32),
            jax.ShapeDtypeStruct((144, 128), BF16),
            jax.ShapeDtypeStruct((72, 128), BF16),
            jax.ShapeDtypeStruct((216, 128), BF16),
            jax.ShapeDtypeStruct((72, 128), BF16),
            jax.ShapeDtypeStruct((2, 2, 2, 128, 512), BF16),
        ),
        in_specs=[vmem] * len(args),
        out_specs=(vmem,) * 7,
        scratch_shapes=[
            pltpu.VMEM((channels * rows, strip + 256), F32),
            pltpu.VMEM((10 * height, n_z * strip + 256), F32),
            pltpu.VMEM((n_z, 10 * height, strip + 256), F32),
            dma((2,)), dma((2,)), dma((2,)), dma((2,)), dma((n_z,)), dma((n_z,)), dma,
        ],
        compiler_params=pltpu.CompilerParams(
            collective_id=2, has_side_effects=True, vmem_limit_bytes=48 * 1024 * 1024
        ),
    )(*args)


def local(
    coarse, target, noise, land_mask, level_index,
    frozen_first, frozen_middle, frozen_last, diffuse_in, diffuse_down, diffuse_up, diffuse_out,
):
    n_lat = lax.axis_size("lat")
    rows = coarse.shape[1]
    strip = coarse.shape[2]
    height, breadth = target.shape[1], target.shape[2]
    wide, packed, wfirst, wlast, win, wout, weff = exchange(
        n_lat, lax.axis_size("lon"),
        (
            coarse, target, noise, land_mask, level_index,
            frozen_first, frozen_last, diffuse_in, diffuse_up, diffuse_out,
        ),
    )
    span = strip // 2 + 2 * HALF
    scale = 1.0 / (target.shape[0] * math.sqrt(height * n_lat * breadth * lax.axis_size("lon")))
    n_pair = lax.axis_size("lon") // 2
    chunk = -(-AT_END // (2 * n_pair * n_lat * 16)) * 16
    total = 2 * n_pair * n_lat * chunk
    den, grads = compute(
        rows, span, scale, total,
        (wide, packed, wfirst, wlast, win, wout, weff, frozen_middle, diffuse_down),
    )
    den, grads = reduce_all(den, grads, n_pair, n_lat, chunk, height)
    den = den[:, :, :, :4, HALF : span - HALF]
    den = den.transpose(3, 1, 0, 4, 2).reshape(4, height, breadth)
    gdown = grads[:AT_UP].reshape(3, 3, 256, 128).astype(F32)
    gup = grads[AT_UP:AT_IN].reshape(3, 3, 2, 128, 128).transpose(0, 1, 3, 2, 4).reshape(3, 3, 128, 256).astype(F32)
    gin = grads[AT_IN:AT_LAST].reshape(3, 3, 24, 128)[:, :, : diffuse_in.shape[3]].transpose(0, 1, 3, 2).astype(F32)
    glast = grads[AT_LAST:AT_END].reshape(3, 3, 8, 128)[:, :, :4].astype(F32)
    return den, gin, gdown, gup, glast


def reduce_kernel(
    n_pair, n_z, chunk, height,
    den_ref, x_ref, den_out, out_ref,
    got1, give2, got2, acc, give3, got3,
    ss1, rs1, ss2, rs2, ss3, rs3, ss4, rs4, ss5, rs5, ss6, rs6, ssd, rsd, own_sem,
):
    lon = lax.axis_index("lon")
    z = lax.axis_index("lat")
    core = lax.rem(lon, 2)
    me = lon // 2
    block = n_z * chunk
    half = n_pair * block
    peer = (me * 2 + 1 - core, z)

    def chip(d):
        return lax.rem(me + d, n_pair)

    def plane(d):
        return lax.rem(z + d, n_z)

    def at_chip(k):
        return (k * 2 + core, z)

    def at_plane(k):
        return (lon, k)

    def rows_at(start, count):
        return pl.ds(pl.multiple_of(start, 16), count)

    def copy(src, dst, send, recv, where):
        return pltpu.make_async_remote_copy(
            src_ref=src, dst_ref=dst, send_sem=send, recv_sem=recv,
            device_id=where, device_id_type=pl.DeviceIdType.MESH,
        )

    barrier = pltpu.get_barrier_semaphore()
    partners = [peer] + [at_chip(chip(d)) for d in range(1, n_pair)] + [at_plane(plane(d)) for d in range(1, n_z)]
    for where in partners:
        pl.semaphore_signal(barrier, inc=1, device_id=where, device_id_type=pl.DeviceIdType.MESH)
    pl.semaphore_wait(barrier, len(partners))

    sent = []

    def start(c):
        c.start()
        sent.append(c)

    chips = list(range(1, n_pair)) + [0]
    planes_on = list(range(1, n_z)) + [0]
    pieces = {}
    for d in planes_on:
        for e in chips:
            at = chip(e) * block + plane(d) * chunk
            c = copy(
                x_ref.at[rows_at((1 - core) * half + at, chunk)],
                got1.at[rows_at(at, chunk)], ss1.at[d, e], rs1.at[d, e], peer,
            )
            start(c)
            pieces[d, e] = c
    for d in range(1, n_z):
        k = plane(d)
        start(copy(den_ref.at[pl.ds(k * height, height)], den_out.at[z], ssd.at[d], rsd.at[d], at_plane(k)))
    own = pltpu.make_async_copy(den_ref.at[pl.ds(z * height, height)], den_out.at[z], own_sem)
    own.start()

    def add_pair(d):
        for e in chips:
            pieces[d, e].wait_recv()
            at = chip(e) * block + plane(d) * chunk
            pair = x_ref[rows_at(core * half + at, chunk), :] + got1[rows_at(at, chunk), :]
            if e:
                give2[d, e] = pair.astype(BF16)
                start(copy(give2.at[d, e], got2.at[d, e], ss2.at[d, e], rs2.at[d, e], at_chip(chip(e))))
            else:
                acc[d] = pair

    def add_plane(d):
        for e in range(1, n_pair):
            copy(give2.at[d, e], got2.at[d, e], ss2.at[d, e], rs2.at[d, e], at_chip(chip(e))).wait_recv()
        s = acc[d]
        for e in range(1, n_pair):
            s = s + got2[d, e].astype(F32)
        if d:
            give3[d] = s.astype(BF16)
            start(copy(give3.at[d], got3.at[d], ss3.at[d], rs3.at[d], at_plane(plane(d))))
        return s

    for n, d in enumerate(planes_on):
        add_pair(d)
        if n:
            add_plane(planes_on[n - 1])
    s = add_plane(0)
    for d in range(1, n_z):
        copy(give3.at[d], got3.at[d], ss3.at[d], rs3.at[d], at_plane(plane(d))).wait_recv()
        s = s + got3[d].astype(F32)

    def place(k, p):
        return out_ref.at[rows_at(core * half + k * block + p * chunk, chunk)]

    out_ref[rows_at(core * half + me * block + z * chunk, chunk), :] = s.astype(BF16)
    mine = place(me, z)
    for d in range(1, n_z):
        start(copy(mine, mine, ss4.at[d], rs4.at[d], at_plane(plane(d))))

    def pass_on(d):
        ref = place(me, plane(d))
        for e in range(1, n_pair):
            start(copy(ref, ref, ss5.at[d, e], rs5.at[d, e], at_chip(chip(e))))
        start(copy(ref, ref, ss6.at[d, 0], rs6.at[d, 0], peer))

    def arrived(d):
        for e in range(1, n_pair):
            ref = place(chip(n_pair - e), plane(d))
            copy(ref, ref, ss5.at[d, e], rs5.at[d, e], at_chip(chip(e))).wait_recv()
            start(copy(ref, ref, ss6.at[d, e], rs6.at[d, e], peer))

    pass_on(0)
    for d in range(1, n_z):
        ref = place(me, plane(d))
        copy(ref, ref, ss4.at[n_z - d], rs4.at[n_z - d], at_plane(plane(d))).wait_recv()
        pass_on(d)
        arrived(d - 1)
    arrived(n_z - 1)

    def from_peer(k, p):
        return out_ref.at[rows_at((1 - core) * half + k * block + p * chunk, chunk)]

    for d in range(n_z):
        for e in range(n_pair):
            ref = from_peer(chip(n_pair - e), plane(d))
            copy(ref, ref, ss6.at[d, e], rs6.at[d, e], peer).wait_recv()
    for d in range(1, n_z):
        k = plane(n_z - d)
        copy(den_ref.at[pl.ds(0, height)], den_out.at[k], ssd.at[d], rsd.at[d], at_plane(k)).wait_recv()
    own.wait()
    for c in sent:
        c.wait_send()


def reduce_all(den, grads, n_pair, n_lat, chunk, height):
    block = n_lat * chunk
    vmem = pl.BlockSpec(memory_space=pltpu.VMEM)
    dma = pltpu.SemaphoreType.DMA
    sems = [(n_lat, n_pair)] * 4 + [(n_lat,)] * 4 + [(n_lat, n_pair)] * 4 + [(n_lat,)] * 2
    return pl.pallas_call(
        functools.partial(reduce_kernel, n_pair, n_lat, chunk, height),
        out_shape=(
            jax.ShapeDtypeStruct((n_lat, height) + den.shape[1:], F32),
            jax.ShapeDtypeStruct(grads.shape, BF16),
        ),
        in_specs=[vmem] * 2,
        out_specs=(vmem,) * 2,
        scratch_shapes=[
            pltpu.VMEM((n_pair * block, 128), F32),
            pltpu.VMEM((n_lat, n_pair, chunk, 128), BF16),
            pltpu.VMEM((n_lat, n_pair, chunk, 128), BF16),
            pltpu.VMEM((n_lat, chunk, 128), F32),
            pltpu.VMEM((n_lat, chunk, 128), BF16),
            pltpu.VMEM((n_lat, chunk, 128), BF16),
        ]
        + [dma(s) for s in sems]
        + [dma],
        compiler_params=pltpu.CompilerParams(
            collective_id=1, has_side_effects=True, vmem_limit_bytes=48 * 1024 * 1024
        ),
    )(den, grads)


def solution(mesh):
    return jax.shard_map(
        local,
        mesh=mesh,
        in_specs=(
            P(None, None, ("lon", "lat")),
            P(None, "lat", "lon"),
            P(None, "lat", "lon"),
            P("lat", "lon"),
            P("lat", "lon"),
            P(), P(), P(), P(), P(), P(), P(),
        ),
        out_specs=(P(None, "lat", "lon"), P(), P(), P(), P()),
        check_vma=False,
    )
```

```python
import functools
import math

import jax
import jax.numpy as jnp
from jax import lax
from jax.experimental import pallas as pl
from jax.experimental.pallas import tpu as pltpu
from jax.sharding import PartitionSpec as P

LEVELS = 32
EDGE = 16
HALF = EDGE // 2
AT_UP = 9 * 256
AT_IN = AT_UP + 9 * 256
AT_LAST = AT_IN + 216
AT_END = AT_LAST + 72
GROUPS = (((0,), (1, 2)), ((0, 1), (2,)))
F32 = jnp.float32
BF16 = jnp.bfloat16


def dot_nt(x, y):
    return lax.dot_general(x, y, (((1,), (1,)), ((), ())), preferred_element_type=F32)


def dot_tn(x, y):
    return lax.dot_general(x, y, (((0,), (0,)), ((), ())), preferred_element_type=F32)


def dot_nn(x, y):
    return jnp.dot(x, y, preferred_element_type=F32)


def sigmoid(v):
    return 1.0 / (1.0 + jnp.exp(-v))


def roll(x, amount, axis):
    size = x.shape[axis]
    return pltpu.roll(x, amount % size, axis)


def kernel(
    rows, span, scale,
    coarse_ref, packed_ref, first_ref, last_ref, in_ref, out_ref, weff, middle_ref, down_ref,
    den_ref, grad_ref,
    fine, pre_a, act_a, pool, pre_b, deep, pre_c, act_c, back, net,
):
    cells = rows * span
    low = rows // 2
    lcells = low * span
    lane = lax.broadcasted_iota(jnp.int32, (1, cells), 1)
    row_of = lane // span
    col_of = lane - row_of * span
    own = (col_of >= HALF) & (col_of < span - HALF)
    col_l = lax.broadcasted_iota(jnp.int32, (lcells, 1), 0) % span
    own_l = (col_l >= HALF) & (col_l < span - HALF)
    col_f = lax.broadcasted_iota(jnp.int32, (cells, 1), 0) % span
    own_f = (col_f >= HALF) & (col_f < span - HALF)

    def row_shift(x, step):
        if step == 0:
            return x
        ok = (row_of + step >= 0) & (row_of + step < rows)
        return jnp.where(ok, roll(x, -step * span, 1), 0.0)

    def col_sources(even, odd):
        return [roll(odd, 1, 1), even, odd, roll(even, -1, 1)]

    def taps(even, odd):
        src = col_sources(even, odd)
        return [[row_shift(s, a - 1) for s in src] for a in range(3)]

    def unfold(table, plane):
        parts = [table[a][plane + b] for a in range(3) for b in range(3)]
        return jnp.concatenate(parts, 0).astype(BF16)

    def unfold_back(table, plane):
        parts = [table[2 - a][plane + 2 - b] for a in range(3) for b in range(3)]
        return jnp.concatenate(parts, 0).astype(BF16)

    def narrow_conv(x_even, x_odd, w):
        ys = (dot_nt(w, x_even), dot_nt(w, x_odd))
        outs = []
        for plane in range(2):
            total = None
            for a in range(3):
                part = None
                for b in range(3):
                    k = plane + b
                    y = ys[(k + 1) % 2][(3 * a + b) * 8 : (3 * a + b) * 8 + 8]
                    if k == 0:
                        y = roll(y, 1, 1)
                    if k == 3:
                        y = roll(y, -1, 1)
                    part = y if part is None else part + y
                part = row_shift(part, a - 1)
                total = part if total is None else total + part
            outs.append(total)
        return outs

    def store_fine(even, odd):
        for k, v in enumerate((roll(odd, 1, 0), even, odd, roll(even, -1, 0))):
            fine[span : span + cells, 128 * k : 128 * k + 128] = v.astype(BF16)

    def store_low(ref, v):
        c = v.shape[1]
        for k, s in enumerate((roll(v, 1, 0), v, roll(v, -1, 0))):
            ref[span : span + lcells, c * k : c * k + c] = s.astype(BF16)

    for ref, count in ((fine, rows), (pool, low), (deep, low)):
        zero = jnp.zeros((span, ref.shape[1]), BF16)
        ref[0:span, :] = zero
        ref[(count + 1) * span : (count + 2) * span, :] = zero

    coarse = (coarse_ref[0], coarse_ref[1])
    table = taps(*coarse)
    first = []
    for plane in range(2):
        v = dot_tn(unfold(table, plane), first_ref[...])
        first.append((v * sigmoid(v)).astype(BF16).astype(F32))
    store_fine(*first)
    second = []
    for plane in range(2):
        v = None
        for a in range(3):
            w = jnp.concatenate([middle_ref[a, b] for b in range(3)], 1)
            d = dot_nt(fine[a * span : a * span + cells, 128 * plane : 128 * plane + 384], w)
            v = d if v is None else v + d
        second.append((v * sigmoid(v)).astype(BF16))
    mean = [m.astype(BF16).astype(F32) for m in narrow_conv(second[0], second[1], last_ref[...])]

    residual, noisy, sigma, mixed = [], [], [], []
    used = lax.broadcasted_iota(jnp.int32, (8, cells), 0) < 4
    for plane in range(2):
        sig = packed_ref[plane, 9:10]
        both = packed_ref[plane, 0:8]
        res = both - mean[plane]
        noi = res + sig * roll(both, 4, 0)
        c_in = lax.rsqrt(sig * sig + 0.25)
        scaled = jnp.where(used, (c_in * noi).astype(BF16).astype(F32), 0.0)
        mixed.append(jnp.concatenate([mean[plane] + roll(scaled, 4, 0), coarse[plane]], 0))
        residual.append(res)
        noisy.append(noi)
        sigma.append(sig)
    table = taps(*mixed)
    for plane in range(2):
        net[plane] = unfold(table, plane)
        v = dot_tn(net[plane], in_ref[...])
        pre_a[plane] = v
        act_a[plane] = (v * sigmoid(v)).astype(BF16)

    parts = []
    for i in range(low):
        total = None
        for r in (2 * i, 2 * i + 1):
            for plane in range(2):
                v = act_a[plane, r * span : (r + 1) * span].astype(F32)
                total = v if total is None else total + v
        parts.append(0.25 * total)
    store_low(pool, jnp.concatenate(parts, 0).astype(BF16).astype(F32))
    v = None
    for a in range(3):
        w = jnp.concatenate([down_ref[a, b] for b in range(3)], 1)
        d = dot_nt(pool[a * span : a * span + lcells, :], w)
        v = d if v is None else v + d
    pre_b[...] = v
    store_low(deep, (v * sigmoid(v)).astype(BF16).astype(F32))

    for pr in range(2):
        for pc in range(2):
            v = None
            for rho in range(2):
                at = (pr + rho) * span
                d = dot_nt(deep[at : at + lcells, 256 * pc : 256 * pc + 512], weff[pr, pc, rho])
                v = d if v is None else v + d
            s = v * sigmoid(v)
            for i in range(low):
                r = 2 * i + pr
                here = slice(r * span, (r + 1) * span)
                there = slice(i * span, (i + 1) * span)
                pre_c[pc, here] = v[there]
                act_c[pc, here] = (s[there] + act_a[pc, here].astype(F32)).astype(BF16)

    field = narrow_conv(act_c[0], act_c[1], out_ref[...])
    grad_f = []
    for plane in range(2):
        sig = sigma[plane]
        var = sig * sig + 0.25
        c_out = 0.5 * sig * lax.rsqrt(var)
        den = (0.25 / var) * noisy[plane] + c_out * field[plane]
        for r in range(rows):
            den_ref[r, plane] = den[:, r * span : (r + 1) * span]
        weight = 1.0 + packed_ref[plane, 8:9]
        lam = var / (0.25 * sig * sig)
        loss_grad = 2.0 * scale * weight * lam * (den - residual[plane])
        grad_f.append((c_out * loss_grad).astype(BF16).astype(F32))
    table = taps(*[jnp.where(own, g, 0.0) for g in grad_f])
    grad_ref[AT_LAST : AT_LAST + 72] = dot_nn(unfold_back(table, 0), act_c[0]) + dot_nn(
        unfold_back(table, 1), act_c[1]
    )
    table = taps(*grad_f)
    grad_c = []
    for plane in range(2):
        v = dot_tn(unfold_back(table, plane), out_ref[...])
        back[plane] = v
        pre = pre_c[plane]
        s = sigmoid(pre)
        grad_c.append((v * (s * (1.0 + pre * (1.0 - s)))).astype(BF16).astype(F32))
    store_fine(*grad_c)

    sums = {}
    for pr in range(2):
        for pc in range(2):
            g = jnp.concatenate([grad_c[pc][(2 * i + pr) * span : (2 * i + pr + 1) * span] for i in range(low)], 0)
            g = jnp.where(own_l, g, 0.0).T.astype(BF16)
            for rho in range(2):
                at = (pr + rho) * span
                d = dot_nn(g, deep[at : at + lcells, 256 * pc : 256 * pc + 512])
                for gam in range(2):
                    part = d[:, 256 * gam : 256 * gam + 256]
                    for a in GROUPS[pr][rho]:
                        for b in GROUPS[pc][gam]:
                            for h in range(2):
                                at_up = AT_UP + ((3 * a + b) * 2 + h) * 128
                                piece = part[:, 128 * h : 128 * h + 128]
                                if (a, b) in sums:
                                    piece = grad_ref[at_up : at_up + 128] + piece
                                grad_ref[at_up : at_up + 128] = piece
                            sums[(a, b)] = True

    order = ((1, 1), (0, 1), (1, 0), (0, 0))
    v = None
    for k in range(4):
        pr, rho = ((1, 1), (0, 1), (1, 0), (0, 0))[k]
        x = jnp.concatenate([fine[(2 * i + k) * span : (2 * i + k + 1) * span, :] for i in range(low)], 0)
        w = jnp.concatenate([weff[pr, pc, rho, :, 256 * gam : 256 * gam + 256] for pc, gam in order], 0)
        d = dot_nn(x, w)
        v = d if v is None else v + d
    pre = pre_b[...]
    s = sigmoid(pre)
    grad_b = (v * (s * (1.0 + pre * (1.0 - s)))).astype(BF16).astype(F32)
    store_low(deep, grad_b)
    g = jnp.where(own_l, grad_b, 0.0).T.astype(BF16)
    for a in range(3):
        d = dot_nn(g, pool[a * span : a * span + lcells, :])
        for b in range(3):
            at = (3 * a + b) * 256
            grad_ref[at : at + 256] = d[:, 128 * b : 128 * b + 128]

    v = None
    for a in range(3):
        w = jnp.concatenate([down_ref[a, b] for b in (2, 1, 0)], 0)
        d = dot_nn(deep[(2 - a) * span : (2 - a) * span + lcells, :], w)
        v = d if v is None else v + d
    v = 0.25 * v
    total = None
    for plane in range(2):
        spread = jnp.concatenate([v[(r // 2) * span : (r // 2 + 1) * span] for r in range(rows)], 0)
        pre = pre_a[plane]
        s = sigmoid(pre)
        g = (back[plane] + spread) * (s * (1.0 + pre * (1.0 - s)))
        g = jnp.where(own_f, g, 0.0).astype(BF16)
        d = dot_nn(net[plane], g)
        total = d if total is None else total + d
    grad_ref[AT_IN : AT_IN + 216] = total
    grad_ref[AT_END:] = jnp.zeros((grad_ref.shape[0] - AT_END, 128), F32)


def compute(rows, span, scale, total, args):
    cells = rows * span
    low = rows // 2
    lcells = low * span
    vmem = pl.BlockSpec(memory_space=pltpu.VMEM)
    return pl.pallas_call(
        functools.partial(kernel, rows, span, scale),
        out_shape=(
            jax.ShapeDtypeStruct((rows, 2, 8, span), F32),
            jax.ShapeDtypeStruct((total, 128), F32),
        ),
        in_specs=[vmem] * len(args),
        out_specs=(vmem,) * 2,
        scratch_shapes=[
            pltpu.VMEM((cells + 2 * span, 512), BF16),
            pltpu.VMEM((2, cells, 128), F32),
            pltpu.VMEM((2, cells, 128), BF16),
            pltpu.VMEM((lcells + 2 * span, 384), BF16),
            pltpu.VMEM((lcells, 256), F32),
            pltpu.VMEM((lcells + 2 * span, 768), BF16),
            pltpu.VMEM((2, cells, 128), F32),
            pltpu.VMEM((2, cells, 128), BF16),
            pltpu.VMEM((2, cells, 128), F32),
            pltpu.VMEM((2, 216, cells), BF16),
        ],
        compiler_params=pltpu.CompilerParams(vmem_limit_bytes=63 * 1024 * 1024),
    )(*args)


def exchange_kernel(
    n_z, n_lon, strip, height,
    level_ref, coarse_hbm, target_hbm, noise_hbm, mask_hbm,
    first_hbm, last_hbm, in_hbm, up_hbm, out_hbm,
    coarse_out, packed_out, wfirst, wlast, win, wout, weff,
    wide, tile, got, ss_c, rs_c, ss_t, rs_t, ss_z, rs_z, own_sem,
    coarse_ref, target_ref, noise_ref, mask_ref, first_ref, last_ref, in_ref, up_ref, out_ref, load_sem,
):
    lon = lax.axis_index("lon")
    z = lax.axis_index("lat")
    rows = n_z * height
    span = strip // 2 + 2 * HALF
    breadth = n_z * strip
    pairs = (
        (coarse_hbm, coarse_ref), (target_hbm, target_ref), (noise_hbm, noise_ref), (mask_hbm, mask_ref),
        (first_hbm, first_ref), (in_hbm, in_ref), (last_hbm, last_ref), (out_hbm, out_ref), (up_hbm, up_ref),
    )
    loads = [pltpu.make_async_copy(src, dst, load_sem.at[i]) for i, (src, dst) in enumerate(pairs)]
    for c in loads:
        c.start()
    strips = n_lon * n_z
    mine = lon * n_z + z

    def of_strip(s):
        return (s // n_z, lax.rem(s, n_z))

    def of_lon(q):
        return (lax.rem(q + n_lon, n_lon), z)

    def plane(d):
        return lax.rem(z + d, n_z)

    def at_plane(k):
        return (lon, k)

    next_strip = of_strip(lax.rem(mine + 1, strips))
    last_strip = of_strip(lax.rem(mine + strips - 1, strips))
    next_lon, last_lon = of_lon(lon + 1), of_lon(lon - 1)

    def copy(src, dst, send, recv, where):
        return pltpu.make_async_remote_copy(
            src_ref=src, dst_ref=dst, send_sem=send, recv_sem=recv,
            device_id=where, device_id_type=pl.DeviceIdType.MESH,
        )

    barrier = pltpu.get_barrier_semaphore()
    partners = [next_strip, last_strip, next_lon, last_lon] + [at_plane(plane(d)) for d in range(1, n_z)]
    for where in partners:
        pl.semaphore_signal(barrier, inc=1, device_id=where, device_id_type=pl.DeviceIdType.MESH)

    level = level_ref[...].astype(F32)
    sigma = 0.02 * jnp.exp(level * (math.log(4000.0) / (LEVELS - 1)))
    body = slice(128, 128 + breadth)
    for c in range(5):
        loads[c].wait()
    for r in range(height):
        at = 10 * r
        for c in range(4):
            tile[at + c : at + c + 1, body] = target_ref[c, r : r + 1, :]
            tile[at + 4 + c : at + 5 + c, body] = noise_ref[c, r : r + 1, :]
        tile[at + 8 : at + 9, body] = mask_ref[r : r + 1, :].astype(F32)
        tile[at + 9 : at + 10, body] = jnp.broadcast_to(sigma, (1, breadth))
    for c in range(coarse_ref.shape[0]):
        wide[c * rows : (c + 1) * rows, 128 : 128 + strip] = coarse_ref[c].astype(F32)
    pl.semaphore_wait(barrier, len(partners))

    sent = []

    def start(c):
        c.start()
        sent.append(c)
        return c

    right_t = start(copy(tile.at[:, pl.ds(breadth, 128)], tile.at[:, pl.ds(0, 128)], ss_t.at[0], rs_t.at[0], next_lon))
    left_t = start(copy(tile.at[:, pl.ds(128, 128)], tile.at[:, pl.ds(breadth + 128, 128)], ss_t.at[1], rs_t.at[1], last_lon))
    right_c = start(copy(wide.at[:, pl.ds(strip, 128)], wide.at[:, pl.ds(0, 128)], ss_c.at[0], rs_c.at[0], next_strip))
    left_c = start(copy(wide.at[:, pl.ds(128, 128)], wide.at[:, pl.ds(strip + 128, 128)], ss_c.at[1], rs_c.at[1], last_strip))

    def tall(ref, channels):
        parts = []
        for a in range(3):
            for b in range(3):
                t = ref[a, b].astype(F32)
                parts.append(t)
                if channels > t.shape[0]:
                    parts.append(jnp.zeros((channels - t.shape[0], t.shape[1]), F32))
        return jnp.concatenate(parts, 0).astype(BF16)

    def flat(ref):
        parts = []
        for a in range(3):
            for b in range(3):
                t = ref[a, b].astype(F32)
                parts += [t, jnp.zeros((8 - t.shape[0], t.shape[1]), F32)]
        return jnp.concatenate(parts, 0).astype(BF16)

    wfirst[...] = tall(first_ref, 16)
    right_t.wait_recv()
    left_t.wait_recv()

    def window(k):
        return tile.at[:, pl.ds(pl.multiple_of(k * strip, 128), strip + 256)]

    for d in range(1, n_z):
        start(copy(window(plane(d)), got.at[z], ss_z.at[d], rs_z.at[d], at_plane(plane(d))))
    own = pltpu.make_async_copy(window(z), got.at[z], own_sem)
    own.start()

    for c in loads[5:]:
        c.wait()
    win[...] = tall(in_ref, 24)
    wlast[...] = flat(last_ref)
    wout[...] = flat(out_ref)
    for pr in range(2):
        for pc in range(2):
            for rho in range(2):
                for gam in range(2):
                    w = None
                    for a in GROUPS[pr][rho]:
                        for b in GROUPS[pc][gam]:
                            u = up_ref[a, b].astype(F32)
                            w = u if w is None else w + u
                    weff[pr, pc, rho, :, 256 * gam : 256 * gam + 256] = w.astype(BF16)

    shape = (strip + 256, 2 * span)
    source = lax.broadcasted_iota(jnp.int32, shape, 0)
    slot = lax.broadcasted_iota(jnp.int32, shape, 1)
    parity = (slot >= span).astype(jnp.int32)
    wanted = 128 - EDGE + 2 * (slot - parity * span) + parity
    pick = (source == wanted).astype(F32)

    right_c.wait_recv()
    left_c.wait_recv()
    split = dot_nn(wide[...].astype(BF16), pick.astype(BF16)).reshape(coarse_ref.shape[0], rows, 2 * span)
    coarse_out[...] = jnp.zeros(coarse_out.shape, F32)
    for r in range(rows):
        for p in range(2):
            part = split[:, r, p * span : (p + 1) * span]
            coarse_out[p, 0 : coarse_ref.shape[0], r * span : (r + 1) * span] = part
    for d in range(1, n_z):
        k = plane(n_z - d)
        copy(window(k), got.at[k], ss_z.at[d], rs_z.at[d], at_plane(k)).wait_recv()
    own.wait()
    packed_out[...] = jnp.zeros(packed_out.shape, F32)
    fields = got[...].reshape(n_z * 10 * height, strip + 256)
    total, rest = None, fields
    for _ in range(3):
        term = rest.astype(BF16)
        rest = rest - term.astype(F32)
        part = dot_nn(term, pick.astype(BF16))
        total = part if total is None else total + part
    total = total.reshape(n_z, 10 * height, 2 * span)
    for k in range(n_z):
        for r in range(height):
            here = slice((k * height + r) * span, (k * height + r + 1) * span)
            for p in range(2):
                cut = slice(p * span, (p + 1) * span)
                packed_out[p, 0:10, here] = total[k, 10 * r : 10 * r + 10, cut]
    for c in sent:
        c.wait_send()


def exchange(n_z, n_lon, args):
    coarse, target = args[1], args[2]
    channels, rows, strip = coarse.shape
    height = target.shape[1]
    cells = rows * (strip // 2 + 2 * HALF)
    vmem = pl.BlockSpec(memory_space=pltpu.VMEM)
    dma = pltpu.SemaphoreType.DMA
    return pl.pallas_call(
        functools.partial(exchange_kernel, n_z, n_lon, strip, height),
        out_shape=(
            jax.ShapeDtypeStruct((2, 16, cells), F32),
            jax.ShapeDtypeStruct((2, 16, cells), F32),
            jax.ShapeDtypeStruct((144, 128), BF16),
            jax.ShapeDtypeStruct((72, 128), BF16),
            jax.ShapeDtypeStruct((216, 128), BF16),
            jax.ShapeDtypeStruct((72, 128), BF16),
            jax.ShapeDtypeStruct((2, 2, 2, 128, 512), BF16),
        ),
        in_specs=[vmem] + [pl.BlockSpec(memory_space=pltpu.HBM)] * (len(args) - 1),
        out_specs=(vmem,) * 7,
        scratch_shapes=[
            pltpu.VMEM((channels * rows, strip + 256), F32),
            pltpu.VMEM((10 * height, n_z * strip + 256), F32),
            pltpu.VMEM((n_z, 10 * height, strip + 256), F32),
            dma((2,)), dma((2,)), dma((2,)), dma((2,)), dma((n_z,)), dma((n_z,)), dma,
        ]
        + [pltpu.VMEM(x.shape, x.dtype) for x in args[1:]]
        + [dma((len(args) - 1,))],
        compiler_params=pltpu.CompilerParams(
            collective_id=2, has_side_effects=True, vmem_limit_bytes=63 * 1024 * 1024
        ),
    )(*args)


def local(
    coarse, target, noise, land_mask, level_index,
    frozen_first, frozen_middle, frozen_last, diffuse_in, diffuse_down, diffuse_up, diffuse_out,
):
    n_lat = lax.axis_size("lat")
    rows = coarse.shape[1]
    strip = coarse.shape[2]
    height, breadth = target.shape[1], target.shape[2]
    wide, packed, wfirst, wlast, win, wout, weff = exchange(
        n_lat, lax.axis_size("lon"),
        (
            level_index, coarse, target, noise, land_mask,
            frozen_first.transpose(0, 1, 3, 2), frozen_last, diffuse_in.transpose(0, 1, 3, 2), diffuse_up, diffuse_out,
        ),
    )
    span = strip // 2 + 2 * HALF
    scale = 1.0 / (target.shape[0] * math.sqrt(height * n_lat * breadth * lax.axis_size("lon")))
    n_pair = lax.axis_size("lon") // 2
    chunk = -(-AT_END // (2 * n_pair * n_lat * 16)) * 16
    total = 2 * n_pair * n_lat * chunk
    den, grads = compute(
        rows, span, scale, total,
        (wide, packed, wfirst, wlast, win, wout, weff, frozen_middle, diffuse_down),
    )
    den, grads = reduce_all(den, grads, n_pair, n_lat, chunk, height)
    den = den[:, :, :, :4, HALF : span - HALF]
    den = den.transpose(3, 1, 0, 4, 2).reshape(4, height, breadth)
    gdown = grads[:AT_UP].reshape(3, 3, 256, 128).astype(F32)
    gup = grads[AT_UP:AT_IN].reshape(3, 3, 2, 128, 128).transpose(0, 1, 3, 2, 4).reshape(3, 3, 128, 256).astype(F32)
    gin = grads[AT_IN:AT_LAST].reshape(3, 3, 24, 128)[:, :, : diffuse_in.shape[3]].transpose(0, 1, 3, 2).astype(F32)
    glast = grads[AT_LAST:AT_END].reshape(3, 3, 8, 128)[:, :, :4].astype(F32)
    return den, gin, gdown, gup, glast


def reduce_kernel(
    n_pair, n_z, chunk, height,
    den_ref, x_ref, den_out, out_ref,
    got1, give2, got2, acc, give3, got3,
    ss1, rs1, ss2, rs2, ss3, rs3, ss4, rs4, ss5, rs5, ss6, rs6, ssd, rsd, own_sem,
):
    lon = lax.axis_index("lon")
    z = lax.axis_index("lat")
    core = lax.rem(lon, 2)
    me = lon // 2
    block = n_z * chunk
    half = n_pair * block
    peer = (me * 2 + 1 - core, z)

    def chip(d):
        return lax.rem(me + d, n_pair)

    def plane(d):
        return lax.rem(z + d, n_z)

    def at_chip(k):
        return (k * 2 + core, z)

    def at_plane(k):
        return (lon, k)

    def rows_at(start, count):
        return pl.ds(pl.multiple_of(start, 16), count)

    def copy(src, dst, send, recv, where):
        return pltpu.make_async_remote_copy(
            src_ref=src, dst_ref=dst, send_sem=send, recv_sem=recv,
            device_id=where, device_id_type=pl.DeviceIdType.MESH,
        )

    barrier = pltpu.get_barrier_semaphore()
    partners = [peer] + [at_chip(chip(d)) for d in range(1, n_pair)] + [at_plane(plane(d)) for d in range(1, n_z)]
    for where in partners:
        pl.semaphore_signal(barrier, inc=1, device_id=where, device_id_type=pl.DeviceIdType.MESH)
    pl.semaphore_wait(barrier, len(partners))

    sent = []

    def start(c):
        c.start()
        sent.append(c)

    chips = list(range(1, n_pair)) + [0]
    planes_on = list(range(1, n_z)) + [0]
    pieces = {}
    for d in planes_on:
        for e in chips:
            at = chip(e) * block + plane(d) * chunk
            c = copy(
                x_ref.at[rows_at((1 - core) * half + at, chunk)],
                got1.at[rows_at(at, chunk)], ss1.at[d, e], rs1.at[d, e], peer,
            )
            start(c)
            pieces[d, e] = c
    for d in range(1, n_z):
        k = plane(d)
        start(copy(den_ref.at[pl.ds(k * height, height)], den_out.at[z], ssd.at[d], rsd.at[d], at_plane(k)))
    own = pltpu.make_async_copy(den_ref.at[pl.ds(z * height, height)], den_out.at[z], own_sem)
    own.start()

    def add_pair(d):
        for e in chips:
            pieces[d, e].wait_recv()
            at = chip(e) * block + plane(d) * chunk
            pair = x_ref[rows_at(core * half + at, chunk), :] + got1[rows_at(at, chunk), :]
            if e:
                give2[d, e] = pair.astype(BF16)
                start(copy(give2.at[d, e], got2.at[d, e], ss2.at[d, e], rs2.at[d, e], at_chip(chip(e))))
            else:
                acc[d] = pair

    def add_plane(d):
        for e in range(1, n_pair):
            copy(give2.at[d, e], got2.at[d, e], ss2.at[d, e], rs2.at[d, e], at_chip(chip(e))).wait_recv()
        s = acc[d]
        for e in range(1, n_pair):
            s = s + got2[d, e].astype(F32)
        if d:
            give3[d] = s.astype(BF16)
            start(copy(give3.at[d], got3.at[d], ss3.at[d], rs3.at[d], at_plane(plane(d))))
        return s

    for n, d in enumerate(planes_on):
        add_pair(d)
        if n:
            add_plane(planes_on[n - 1])
    s = add_plane(0)
    for d in range(1, n_z):
        copy(give3.at[d], got3.at[d], ss3.at[d], rs3.at[d], at_plane(plane(d))).wait_recv()
        s = s + got3[d].astype(F32)

    def place(k, p):
        return out_ref.at[rows_at(core * half + k * block + p * chunk, chunk)]

    out_ref[rows_at(core * half + me * block + z * chunk, chunk), :] = s.astype(BF16)
    mine = place(me, z)
    for d in range(1, n_z):
        start(copy(mine, mine, ss4.at[d], rs4.at[d], at_plane(plane(d))))

    def pass_on(d):
        ref = place(me, plane(d))
        for e in range(1, n_pair):
            start(copy(ref, ref, ss5.at[d, e], rs5.at[d, e], at_chip(chip(e))))
        start(copy(ref, ref, ss6.at[d, 0], rs6.at[d, 0], peer))

    def arrived(d):
        for e in range(1, n_pair):
            ref = place(chip(n_pair - e), plane(d))
            copy(ref, ref, ss5.at[d, e], rs5.at[d, e], at_chip(chip(e))).wait_recv()
            start(copy(ref, ref, ss6.at[d, e], rs6.at[d, e], peer))

    pass_on(0)
    for d in range(1, n_z):
        ref = place(me, plane(d))
        copy(ref, ref, ss4.at[n_z - d], rs4.at[n_z - d], at_plane(plane(d))).wait_recv()
        pass_on(d)
        arrived(d - 1)
    arrived(n_z - 1)

    def from_peer(k, p):
        return out_ref.at[rows_at((1 - core) * half + k * block + p * chunk, chunk)]

    for d in range(n_z):
        for e in range(n_pair):
            ref = from_peer(chip(n_pair - e), plane(d))
            copy(ref, ref, ss6.at[d, e], rs6.at[d, e], peer).wait_recv()
    for d in range(1, n_z):
        k = plane(n_z - d)
        copy(den_ref.at[pl.ds(0, height)], den_out.at[k], ssd.at[d], rsd.at[d], at_plane(k)).wait_recv()
    own.wait()
    for c in sent:
        c.wait_send()


def reduce_all(den, grads, n_pair, n_lat, chunk, height):
    block = n_lat * chunk
    vmem = pl.BlockSpec(memory_space=pltpu.VMEM)
    dma = pltpu.SemaphoreType.DMA
    sems = [(n_lat, n_pair)] * 4 + [(n_lat,)] * 4 + [(n_lat, n_pair)] * 4 + [(n_lat,)] * 2
    return pl.pallas_call(
        functools.partial(reduce_kernel, n_pair, n_lat, chunk, height),
        out_shape=(
            jax.ShapeDtypeStruct((n_lat, height) + den.shape[1:], F32),
            jax.ShapeDtypeStruct(grads.shape, BF16),
        ),
        in_specs=[vmem] * 2,
        out_specs=(vmem,) * 2,
        scratch_shapes=[
            pltpu.VMEM((n_pair * block, 128), F32),
            pltpu.VMEM((n_lat, n_pair, chunk, 128), BF16),
            pltpu.VMEM((n_lat, n_pair, chunk, 128), BF16),
            pltpu.VMEM((n_lat, chunk, 128), F32),
            pltpu.VMEM((n_lat, chunk, 128), BF16),
            pltpu.VMEM((n_lat, chunk, 128), BF16),
        ]
        + [dma(s) for s in sems]
        + [dma],
        compiler_params=pltpu.CompilerParams(
            collective_id=1, has_side_effects=True, vmem_limit_bytes=48 * 1024 * 1024
        ),
    )(den, grads)


def solution(mesh):
    return jax.shard_map(
        local,
        mesh=mesh,
        in_specs=(
            P(None, None, ("lon", "lat")),
            P(None, "lat", "lon"),
            P(None, "lat", "lon"),
            P("lat", "lon"),
            P("lat", "lon"),
            P(), P(), P(), P(), P(), P(), P(),
        ),
        out_specs=(P(None, "lat", "lon"), P(), P(), P(), P()),
        check_vma=False,
    )
```
